128 devices in a mesh: rep: 16 (over z, x), tp: 8 (over y, core).
Axes of the slice: x: 4, y: 4, z: 4, core: 2. Of those that a mesh axis runs over, the one named last changes fastest.
Arguments:
- x_in: bfloat16 [512, 16384], P('rep', 'tp'), may hold values from -6 to 6
- z_gate: bfloat16 [512, 16384], P('rep', 'tp'), may hold values from -6 to 6
- conv_state: bfloat16 [512, 3, 16384], P('rep', None, 'tp'), may hold values from -6 to 6
- conv_pool: bfloat16 [512, 3, 16384], P('rep', None, 'tp'), may hold values from -6 to 6
- ssm_state: float32 [512, 16, 16384], P('rep', None, 'tp'), may hold values from -6 to 6
- ssm_pool: float32 [512, 16, 16384], P('rep', None, 'tp'), may hold values from -6 to 6
- conv_weight: bfloat16 [4, 16384], P(None, 'tp'), may hold values from -3 to 3
- conv_bias: float32 [16384], P('tp'), may hold values from -0.5 to 0.5
- x_proj: bfloat16 [16384, 544], P('tp'), may hold values from -0.046875 to 0.046875
- dt_gain: float32 [512], replicated, may hold values from 0.5 to 1.5
- b_gain: float32 [16], replicated, may hold values from 0.5 to 1.5
- c_gain: float32 [16], replicated, may hold values from 0.5 to 1.5
- dt_proj: bfloat16 [512, 16384], P(None, 'tp'), may hold values from -0.25 to 0.25
- dt_bias: float32 [16384], P('tp'), may hold values from -3 to 0
- decay_rate: float32 [16, 16384], P(None, 'tp'), may hold values from 0.5 to 16
- skip: float32 [16384], P('tp'), may hold values from 0.5 to 1.5
- query: bfloat16 [512, 8192], P('rep', 'tp'), may hold values from -16 to 16
- new_kv: bfloat16 [512, 2048], P('rep', 'tp'), may hold values from -6 to 6
- kv_cache: bfloat16 [512, 512, 2048], P('rep', None, 'tp'), may hold values from -16 to 16
- kv_pool: bfloat16 [4096, 16, 2048], P('rep', None, 'tp'), may hold values from -16 to 16
- ctx_len: int32 [512], P('rep'), may hold values from 2 to 512
- row_owner: int32 [512], P('rep'), may hold values from -1 to 15, as said below
- row_pos: int32 [512], P('rep'), may hold values from 0 to 1, as said below
- swap_slot: int32 [16, 16, 2], P('rep'), may hold values from 0 to 31, as said below
- swap_lens: int32 [16, 16, 2], P('rep'), may hold values from 2 to 512
- swap_pages: int32 [16, 16, 2, 32], P('rep'), may hold values from 0 to 255
Outputs:
- mamba_out: bfloat16 [512, 16384], P('rep', 'tp')
- attn_out: bfloat16 [512, 8192], P('rep', 'tp')
- new_ssm: float32 [512, 16, 16384], P('rep', None, 'tp')
- new_conv: bfloat16 [512, 3, 16384], P('rep', None, 'tp')
The draws below stay inside these ranges and needn't reach their ends.
Inputs may be any that keep to these rules, and one draw needn't show every extreme that they name: -1 marks a resident request; otherwise the group along rep whose pool holds it. Of one group's rows at most 2 name the same owner, and the pairs (row_owner, row_pos) of one group's resumed rows are distinct; in every draw some group resumes 2 requests from every owner. A resumed request of group g with owner o is entry [o, g, row_pos] of the owner's lists; entries that no request names are unused. `swap_slot`: slots of one owner are distinct. `swap_pages`: only the first ceil(length / 16) pages of a request are read; pages may be shared.
All inputs are finite; a program needn't handle non-finite values.
Results may differ from the reference program's by a relative error of at most 0.013.
Values may be sent and summed in bfloat16 or wider, within the bound.
No kernel may reach another device: no remote copies, remote signals or barrier semaphores. Data moves between devices by JAX's collectives and lax.ppermute only.
A program may use at most 128 MiB of HBM per device.

```python
import math
import jax
import jax.numpy as jnp
from jax import lax

E = 16384
N_STATE = 16
DT_RANK = 512
KCONV = 4
HQ = 64
KVH = 8
HD = 128
ROWS = 32
CTX = 512
PAGE = 16
CAP = 2
POOL_PAGES = 256
PAGES = 32
PEERS = 16
SLOTS = 32
SLOTS_ALL = 512
PAGES_ALL = 4096
NREQ = 512
N_REP = 16


def route_counts(key):
    count_key = jax.random.fold_in(key, 101)
    full_key = jax.random.fold_in(key, 102)
    counts = jax.random.randint(count_key, (PEERS, PEERS), 0, CAP + 1)
    full_peer = jax.random.randint(full_key, (), 0, PEERS)
    counts = jnp.where(jnp.arange(PEERS)[None, :] == full_peer, CAP, counts)
    return (counts, full_peer)


def assign_rows(key):
    counts, full_peer = route_counts(key)
    entry_index = jnp.arange(PEERS * CAP)
    entry_owner = entry_index // CAP
    entry_place = entry_index % CAP
    valid = entry_place[None, :] < counts.T[:, entry_owner]
    ranking = jnp.cumsum(valid.astype(jnp.int32), axis=1) - 1
    perm_keys = jax.random.split(jax.random.fold_in(key, 103), PEERS)
    row_perms = jax.vmap(lambda perm_key: jax.random.permutation(perm_key, ROWS))(perm_keys)
    target = jnp.where(valid, jnp.take_along_axis(row_perms, jnp.clip(ranking, 0, ROWS - 1), axis=1), ROWS)
    peer_index = jnp.broadcast_to(jnp.arange(PEERS)[:, None], target.shape)
    owner_values = jnp.broadcast_to(entry_owner[None, :], target.shape).astype(jnp.int32)
    place_values = jnp.broadcast_to(entry_place[None, :], target.shape).astype(jnp.int32)
    owners = jnp.full((PEERS, ROWS), -1, jnp.int32).at[peer_index, target].set(owner_values, mode='drop')
    places = jnp.zeros((PEERS, ROWS), jnp.int32).at[peer_index, target].set(place_values, mode='drop')
    return (owners.reshape(-1), places.reshape(-1))


def draw_row_owner(key, part):
    owners, places = assign_rows(key)
    return owners.astype(jnp.int32)


def draw_row_pos(key, part):
    owners, places = assign_rows(key)
    return places.astype(jnp.int32)


def draw_swap_slot(key, part):
    key = jax.random.fold_in(key, 5)
    slot_keys = jax.random.split(key, PEERS)
    slot_perms = jax.vmap(lambda slot_key: jax.random.permutation(slot_key, SLOTS))(slot_keys)
    return slot_perms.reshape(PEERS, PEERS, CAP).astype(jnp.int32)


def draw_swap_lens(key, part):
    counts, full_peer = route_counts(key)
    key = jax.random.fold_in(key, 3)
    lengths = jax.random.randint(key, (PEERS, PEERS, CAP), 2, CTX + 1)
    owner_pick = jax.random.randint(jax.random.fold_in(key, 4), (), 0, PEERS)
    lengths = lengths.at[owner_pick, full_peer, 0].set(CTX)
    return lengths.astype(jnp.int32)


def draw_ctx_len(key, part):
    key = jax.random.fold_in(key, 6)
    lengths = jax.random.randint(key, (NREQ,), 2, CTX + 1)
    full_rows = jnp.arange(PEERS) * ROWS + jax.random.randint(jax.random.fold_in(key, 7), (PEERS,), 0, ROWS)
    return lengths.at[full_rows].set(CTX).astype(jnp.int32)


def draw_query(key, part):
    key = jax.random.fold_in(key, 8)
    values = jax.random.normal(key, (NREQ, HQ * HD), jnp.float32)
    return values.astype(jnp.bfloat16)


def kv_values(key, count, tokens):
    values = jax.random.normal(key, (count, tokens, KVH, 2, HD), jnp.float32)
    return values.reshape(count, tokens, KVH * 2 * HD).astype(jnp.bfloat16)


def draw_kv_cache(key, part):
    key = jax.random.fold_in(key, 11)
    return kv_values(key, NREQ, CTX)


def draw_kv_pool(key, part):
    key = jax.random.fold_in(key, 12)
    return kv_values(key, PAGES_ALL, PAGE)


def with_ends(values, own_key, smallest, largest):
    longest = values.shape.index(max(values.shape))
    spots = []
    for shift in (0, 1):
        where = [jax.random.randint(jax.random.fold_in(own_key, axis), (), 0, length) for axis, length in enumerate(values.shape)]
        where[longest] = (where[longest] + shift) % values.shape[longest]
        spots.append(tuple(where))
    return values.at[spots[0]].set(smallest).at[spots[1]].set(largest)


def level_of(stream_key, extent, cuts, least, largest):
    def one(axis_at, blocks):
        draws = jax.random.uniform(jax.random.fold_in(jax.random.fold_in(stream_key, 6), axis_at), (blocks,), jnp.float32, least / len(cuts), largest / len(cuts))
        return jnp.repeat(jnp.exp(draws), extent[axis_at] // blocks).reshape((-1,) + (1,) * (len(extent) - axis_at - 1))

    factor_of = one(*cuts[0])
    for cut in cuts[1:]:
        factor_of = factor_of * one(*cut)
    return factor_of


def gaussian(key, extent, width, limit, cuts=(), held_as=jnp.bfloat16):
    values = width * jax.random.normal(key, extent, jnp.float32)
    if cuts:
        values = values * level_of(key, extent, cuts, -0.22, 0.18)
    return jnp.clip(values, -limit, limit).astype(held_as)


def setup_inputs(seed: int = 0) -> dict:
    key_of = jax.random.split(jax.random.key(seed), 27)
    return {
        "x_in": gaussian(key_of[0], (NREQ, E), 1.0, 6.0, ((0, 16), (1, 8))),
        "z_gate": gaussian(key_of[1], (NREQ, E), 1.0, 6.0, ((0, 16), (1, 8))),
        "conv_state": gaussian(key_of[2], (NREQ, KCONV - 1, E), 1.0, 6.0, ((0, 16), (2, 8))),
        "conv_pool": gaussian(key_of[3], (SLOTS_ALL, KCONV - 1, E), 1.0, 6.0, ((0, 16), (2, 8))),
        "ssm_state": gaussian(key_of[4], (NREQ, N_STATE, E), 1.0, 6.0, ((0, 16), (2, 8)), jnp.float32),
        "ssm_pool": gaussian(key_of[5], (SLOTS_ALL, N_STATE, E), 1.0, 6.0, ((0, 16), (2, 8)), jnp.float32),
        "conv_weight": gaussian(key_of[6], (KCONV, E), KCONV ** -0.5, 3.0, ((1, 8),)),
        "conv_bias": jnp.clip(jax.random.uniform(key_of[7], (E,), jnp.float32, -0.5, 0.5) * level_of(key_of[7], (E,), ((0, 8),), -0.4, 0.0), -0.5, 0.5),
        "x_proj": gaussian(key_of[8], (E, DT_RANK + 2 * N_STATE), E ** -0.5, 0.046875, ((0, 8),)),
        "dt_gain": jnp.clip(jax.random.uniform(key_of[9], (DT_RANK,), jnp.float32, 0.5, 1.5), 0.5, 1.5),
        "b_gain": jnp.clip(jax.random.uniform(key_of[10], (N_STATE,), jnp.float32, 0.5, 1.5), 0.5, 1.5),
        "c_gain": jnp.clip(jax.random.uniform(key_of[11], (N_STATE,), jnp.float32, 0.5, 1.5), 0.5, 1.5),
        "dt_proj": gaussian(key_of[12], (DT_RANK, E), DT_RANK ** -0.5, 0.25, ((1, 8),)),
        "dt_bias": jnp.clip(-3.0 + 3.0 * jax.random.uniform(key_of[13], (E,), jnp.float32) ** level_of(key_of[13], (E,), ((0, 8),), -0.2, 0.2), -3.0, 0.0),
        "decay_rate": jnp.clip(jnp.exp(math.log(16.0) - 3.465736 * jax.random.uniform(key_of[14], (N_STATE, E), jnp.float32) ** level_of(key_of[14], (N_STATE, E), ((1, 8),), -0.2, 0.2)), 0.5, 16.0),
        "skip": jnp.clip(0.5 + 1.0 * jax.random.uniform(key_of[15], (E,), jnp.float32) ** level_of(key_of[15], (E,), ((0, 8),), -0.2, 0.2), 0.5, 1.5),
        "query": draw_query(jax.random.fold_in(key_of[26], 71), 0),
        "new_kv": gaussian(key_of[17], (NREQ, 2 * KVH * HD), 1.0, 6.0, ((0, 16), (1, 8))),
        "kv_cache": draw_kv_cache(jax.random.fold_in(key_of[26], 71), 0),
        "kv_pool": draw_kv_pool(jax.random.fold_in(key_of[26], 71), 0),
        "ctx_len": draw_ctx_len(jax.random.fold_in(key_of[26], 71), 0),
        "row_owner": draw_row_owner(jax.random.fold_in(key_of[26], 71), 0),
        "row_pos": draw_row_pos(jax.random.fold_in(key_of[26], 71), 0),
        "swap_slot": draw_swap_slot(jax.random.fold_in(key_of[26], 71), 0),
        "swap_lens": draw_swap_lens(jax.random.fold_in(key_of[26], 71), 0),
        "swap_pages": with_ends(jax.random.randint(key_of[25], (PEERS, PEERS, CAP, PAGES), 0, POOL_PAGES), jax.random.fold_in(key_of[25], 1), 0, POOL_PAGES - 1).astype(jnp.int32),
    }


def attend_block(query_heads, context, ctx_lengths):
    item_count = query_heads.shape[0]
    kv_heads = query_heads.shape[1]
    head_width = query_heads.shape[3]
    kv_pairs = context.astype(jnp.float32).reshape(item_count, context.shape[1], kv_heads, 2, head_width)
    key_rows = kv_pairs[:, :, :, 0, :]
    value_rows = kv_pairs[:, :, :, 1, :]
    score_block = jnp.einsum('nkgd,ntkd->nkgt', query_heads, key_rows) * (1.0 / math.sqrt(head_width))
    live_mask = (jnp.arange(context.shape[1])[None, :] < ctx_lengths[:, None])[:, None, None, :]
    masked = jnp.where(live_mask, score_block, -1e+30)
    score_top = lax.optimization_barrier(jnp.max(masked, axis=-1))
    prob_weights = jnp.where(live_mask, jnp.exp(masked - score_top[..., None]), 0.0).astype(jnp.bfloat16)
    prob_float = prob_weights.astype(jnp.float32)
    prob_total = lax.optimization_barrier(jnp.sum(prob_float, axis=-1))
    attn_mix = jnp.einsum('nkgt,ntkd->nkgd', prob_float, value_rows)
    return (attn_mix, score_top, prob_total)

def finish(query_heads, new_pairs, attn_mix, score_top, prob_total):
    item_count, kv_heads, q_groups, head_width = query_heads.shape
    kv_pairs = new_pairs.astype(jnp.float32).reshape(item_count, kv_heads, 2, head_width)
    new_score = jnp.einsum('nkgd,nkd->nkg', query_heads, kv_pairs[:, :, 0, :]) * (1.0 / math.sqrt(head_width))
    score_peak = jnp.maximum(score_top, new_score)
    old_scale = jnp.exp(score_top - score_peak)
    new_scale = jnp.exp(new_score - score_peak)
    numerator = attn_mix * old_scale[..., None] + new_scale[..., None] * kv_pairs[:, :, None, 1, :]
    result = numerator / (prob_total * old_scale + new_scale)[..., None]
    return result.reshape(item_count, -1).astype(jnp.bfloat16)

def rms_scaled(values, gain):
    return (values * lax.rsqrt(lax.optimization_barrier(jnp.mean(values * values, axis=-1, keepdims=True)) + 1e-06) * gain).astype(jnp.bfloat16)

def reference(x_in, z_gate, conv_state, conv_pool, ssm_state, ssm_pool, conv_weight, conv_bias, x_proj, dt_gain, b_gain, c_gain, dt_proj, dt_bias, decay_rate, skip, query, new_kv, kv_cache, kv_pool, ctx_len, row_owner, row_pos, swap_slot, swap_lens, swap_pages):
    group_count = N_REP

    def by_group(array):
        return array.reshape((group_count, array.shape[0] // group_count) + array.shape[1:])

    def one_group(group_item):
        group, x_rows, z_rows, conv_rows, ssm_rows, query_rows, new_rows, cache_rows, len_rows, owner_rows, pos_rows = group_item
        resumed = owner_rows >= 0
        owner_rank = jnp.maximum(owner_rows, 0).astype(jnp.int32)
        slot_index = (owner_rank * SLOTS + swap_slot[owner_rank, group, pos_rows]).astype(jnp.int32)
        prev_conv = jnp.where(resumed[:, None, None], conv_pool[slot_index], conv_rows)
        prev_ssm = jnp.where(resumed[:, None, None], ssm_pool[slot_index], ssm_rows)
        conv_window = jnp.concatenate([prev_conv, x_rows[:, None, :]], axis=1)
        conv_sum = lax.optimization_barrier(jnp.sum(conv_window.astype(jnp.float32) * conv_weight.astype(jnp.float32)[None], axis=1)) + conv_bias
        mixed_in = jax.nn.silu(conv_sum).astype(jnp.bfloat16)
        proj = jnp.dot(mixed_in, x_proj, preferred_element_type=jnp.float32)
        dt_normed = rms_scaled(proj[:, :DT_RANK], dt_gain)
        dt_step = jax.nn.softplus(jnp.dot(dt_normed, dt_proj, preferred_element_type=jnp.float32) + dt_bias)
        inject = rms_scaled(proj[:, DT_RANK:DT_RANK + N_STATE], b_gain).astype(jnp.float32)
        read_out = rms_scaled(proj[:, DT_RANK + N_STATE:], c_gain).astype(jnp.float32)
        signal = mixed_in.astype(jnp.float32)
        new_state = jnp.exp(-dt_step[:, None, :] * decay_rate[None]) * prev_ssm + (dt_step * signal)[:, None, :] * inject[:, :, None]
        mamba_rows = ((lax.optimization_barrier(jnp.sum(read_out[:, :, None] * new_state, axis=1)) + skip * signal) * jax.nn.silu(z_rows.astype(jnp.float32))).astype(jnp.bfloat16)
        page_index = (owner_rank[:, None] * POOL_PAGES + swap_pages[owner_rank, group, pos_rows]).astype(jnp.int32)
        remote = kv_pool[page_index].reshape(ROWS, CTX, kv_pool.shape[2])
        context = jnp.where(resumed[:, None, None], remote, cache_rows)
        ctx_lengths = jnp.where(resumed, swap_lens[owner_rank, group, pos_rows], len_rows)
        query_heads = query_rows.astype(jnp.float32).reshape(ROWS, KVH, HQ // KVH, HD)
        attn_mix, score_top, prob_total = attend_block(query_heads, context, ctx_lengths)
        attn_rows = finish(query_heads, new_rows, attn_mix, score_top, prob_total)
        return (mamba_rows, attn_rows, new_state, conv_window[:, 1:])
    mamba_all, attn_all, state_all, conv_all = lax.map(one_group, (jnp.arange(group_count).astype(jnp.int32), by_group(x_in), by_group(z_gate), by_group(conv_state), by_group(ssm_state), by_group(query), by_group(new_kv), by_group(kv_cache), by_group(ctx_len), by_group(row_owner), by_group(row_pos)))
    return (mamba_all.reshape(NREQ, E), attn_all.reshape(NREQ, HQ * HD), state_all.reshape(NREQ, N_STATE, E), conv_all.reshape(NREQ, KCONV - 1, E))
```

```python
import functools
import math

import jax
import jax.numpy as jnp
from jax import lax
from jax.experimental import pallas as pl
from jax.experimental.pallas import tpu as pltpu
from jax.sharding import PartitionSpec as P

BF = jnp.bfloat16
F32 = jnp.float32
I32 = jnp.int32
PEERS = 16
CAP = 2
ENT = PEERS * CAP
ROWS = 32
EC = 2048
HALF = EC // 2
NS = 16
RANK = 512
HEADS = 8
HD = 128
CTX = 512
PAGE = 16
POOL = 256
TOK = POOL * PAGE
CHUNK = 256
LOG2E = 1.4426950408889634
LN2 = 0.6931471805599453
NEG = -1e30

VM = pl.BlockSpec(memory_space=pltpu.VMEM)
SM = pl.BlockSpec(memory_space=pltpu.SMEM)
HB = pl.BlockSpec(memory_space=pl.ANY)


def iota(shape, dim):
    return lax.broadcasted_iota(I32, shape, dim)


def params(mib):
    return pltpu.CompilerParams(vmem_limit_bytes=mib * 1024 * 1024)


def cost(flops, byts):
    return pl.CostEstimate(flops=flops, bytes_accessed=byts, transcendentals=0)


def source_of(owner_ref, pos_ref, r):
    owner = owner_ref[r]
    return jnp.where(owner >= 0, owner * CAP + pos_ref[r], -1)


def pack_kernel(slot_ref, owner_ref, pos_ref, conv_ref, query_ref, out_ref, stack, inverse):
    for j in range(3):
        for h in range(2):
            stack[32 * (2 * j + h) : 32 * (2 * j + h) + 32, :] = conv_ref[
                j, :, h * HALF : (h + 1) * HALF
            ]
    stack[192:224, :] = query_ref[...]
    stack[224:256, :] = jnp.zeros((32, HALF), BF)
    for e in range(ENT):
        inverse[e] = -1
    for r in range(ROWS):
        owner = owner_ref[r]

        @pl.when(owner >= 0)
        def _():
            inverse[owner * CAP + pos_ref[r]] = 192 + r

    lane = iota((8, 256), 1)
    part = iota((8, 256), 0)
    tiles = []
    for e in range(ENT):
        slot = slot_ref[0, e % CAP, e // CAP]
        want = jnp.where(part < 6, 32 * part + slot, jnp.where(part == 6, inverse[e], -1))
        tiles.append((lane == want).astype(F32))
    pick = jnp.concatenate(tiles, axis=0).astype(BF)
    packed = jnp.dot(pick, stack[...], preferred_element_type=F32).astype(BF)
    out_ref[...] = packed.reshape(PEERS, 16, HALF)


def pack(slots, owner, pos, conv_pool, query):
    return pl.pallas_call(
        pack_kernel,
        out_shape=jax.ShapeDtypeStruct((PEERS, 16, HALF), BF),
        in_specs=[SM, SM, SM, VM, VM],
        out_specs=VM,
        scratch_shapes=[pltpu.VMEM((256, HALF), BF), pltpu.SMEM((ENT,), I32)],
        compiler_params=params(16),
        cost_estimate=cost(2 * 256 * 256 * HALF, 1 << 20),
        name="pack_first",
    )(slots, owner, pos, conv_pool, query)


def gather_kernel(slot_ref, pool_ref, out_ref, buf, sems):
    def copy(e):
        return pltpu.make_async_copy(
            pool_ref.at[slot_ref[0, e % CAP, e // CAP]], buf.at[e], sems.at[e]
        )

    for e in range(ENT):
        copy(e).start()

    for e in range(ENT):
        copy(e).wait()
        out_ref[e] = buf[e].astype(BF)


def gather_states(slots, ssm_pool):
    return pl.pallas_call(
        gather_kernel,
        out_shape=jax.ShapeDtypeStruct((ENT, NS, EC), BF),
        in_specs=[SM, HB],
        out_specs=VM,
        scratch_shapes=[pltpu.VMEM((ENT, NS, EC), F32), pltpu.SemaphoreType.DMA((ENT,))],
        compiler_params=params(16),
        cost_estimate=cost(1 << 20, 6 << 20),
        name="gather_states",
    )(slots, ssm_pool)


def weigh_kernel(pages_ref, lens_ref, pool_ref, weight_ref, vt_ref, count):
    lens = lens_ref[...]
    full = lens // PAGE
    rest = lens - full * PAGE
    page_id = iota((POOL, 128), 0)
    total = jnp.zeros((POOL, 128), F32)
    last = jnp.full((1, 128), -1, I32)
    for j in range(CTX // PAGE):
        page = pages_ref[j : j + 1, :]
        total += jnp.where(page_id == jnp.where(j < full, page, -1), 1.0, 0.0)
        last = jnp.where(j == full, page, last)
    count[...] = total
    token = iota((PAGE, 128), 0)
    tail = jnp.where(token < rest, 1.0, 0.0)

    def body(p, carry):
        here = jnp.broadcast_to(count[pl.ds(p, 1), :], (PAGE, 128))
        here += jnp.where(last == p, tail, 0.0)
        weight_ref[p] = here.astype(BF)
        return carry

    lax.fori_loop(0, POOL, body, 0, unroll=8)
    for c in range(TOK // CHUNK):
        pages = CHUNK // PAGE
        values = pool_ref[c * pages : (c + 1) * pages, :, HD:].reshape(CHUNK, HD)
        vt_ref[:, c * CHUNK : (c + 1) * CHUNK] = values.astype(F32).T.astype(BF)


def weigh(pages, lens, kv_pool):
    return pl.pallas_call(
        weigh_kernel,
        out_shape=(
            jax.ShapeDtypeStruct((POOL, PAGE, 128), BF),
            jax.ShapeDtypeStruct((HD, TOK), BF),
        ),
        in_specs=[VM, VM, VM],
        out_specs=(VM, VM),
        scratch_shapes=[pltpu.VMEM((POOL, 128), F32)],
        compiler_params=params(16),
        cost_estimate=cost(1 << 20, 6 << 20),
        name="weigh_pool",
    )(pages, lens, kv_pool)


def serve_kernel(recv_ref, pool_ref, weight_ref, vt_ref, out_ref, scores, back):
    lane = iota((ENT, 256), 1)
    pick = (lane == 8 * iota((ENT, 256), 0) + 6).astype(F32).astype(BF)
    recv = recv_ref[...].reshape(256, HALF)
    query = jnp.dot(pick, recv, preferred_element_type=F32).astype(BF)
    query = jnp.concatenate([query[:, h * HD : (h + 1) * HD] for h in range(HEADS)], axis=0)
    scale = LOG2E / math.sqrt(HD)
    pages = CHUNK // PAGE

    def first(c, top):
        keys = pool_ref[pl.ds(c * pages, pages), :, 0:HD].reshape(CHUNK, HD)
        raw = lax.dot_general(keys, query, (((1,), (1,)), ((), ())), preferred_element_type=F32)
        weight = weight_ref[pl.ds(c * pages, pages)].reshape(CHUNK, 128).astype(F32)
        weight = jnp.concatenate([weight, weight], axis=1)
        raw = jnp.where(weight > 0.0, raw * scale, NEG)
        scores[pl.ds(c * CHUNK, CHUNK), :] = raw
        return jnp.maximum(top, jnp.max(raw.reshape(CHUNK // 8, 8, 256), axis=0))

    top = lax.fori_loop(0, TOK // CHUNK, first, jnp.full((8, 256), NEG, F32))
    top = jnp.max(top, axis=0, keepdims=True)

    def second(c, carry):
        total, mix = carry
        raw = scores[pl.ds(c * CHUNK, CHUNK), :]
        weight = weight_ref[pl.ds(c * pages, pages)].reshape(CHUNK, 128).astype(F32)
        weight = jnp.concatenate([weight, weight], axis=1)
        prob = (jnp.exp2(raw - top) * weight).astype(BF)
        total += jnp.sum(prob.astype(F32).reshape(CHUNK // 8, 8, 256), axis=0)
        start = pl.multiple_of(c * CHUNK, CHUNK)
        mix += jnp.dot(vt_ref[:, pl.ds(start, CHUNK)], prob, preferred_element_type=F32)
        return total, mix

    total, mix = lax.fori_loop(
        0, TOK // CHUNK, second, (jnp.zeros((8, 256), F32), jnp.zeros((HD, 256), F32))
    )
    total = jnp.sum(total, axis=0, keepdims=True)
    lse = top * LN2 + jnp.log(total)
    high = lse.astype(BF).astype(F32)
    mid = (lse - high).astype(BF).astype(F32)
    low = lse - high - mid
    row = iota((HD, 256), 0)
    pieces = jnp.where(row < 32, high, jnp.where(row < 64, mid, low))
    mix = (mix * (1.0 / total)).T
    pieces = pieces.T
    for h in range(HEADS):
        back[pl.ds(h, ENT, 16), :] = mix[h * ENT : (h + 1) * ENT, :]
        back[pl.ds(8 + h, ENT, 16), :] = pieces[h * ENT : (h + 1) * ENT, :]
    out_ref[...] = back[...].astype(BF).reshape(PEERS, 32, HD)


def serve(recv, kv_pool, weight, vt):
    return pl.pallas_call(
        serve_kernel,
        out_shape=jax.ShapeDtypeStruct((PEERS, 32, HD), BF),
        in_specs=[VM] * 4,
        out_specs=VM,
        scratch_shapes=[pltpu.VMEM((TOK, 256), F32), pltpu.VMEM((ENT * 16, HD), F32)],
        compiler_params=params(24),
        cost_estimate=cost(4 * TOK * 256 * HD, 6 << 20),
        name="serve_pool",
    )(recv, kv_pool, weight, vt)


BLK = 4


def resident_kernel(len_ref, query_ref, new_ref, cache_ref, mix_ref, lse_ref, score_ref, heads):
    step = pl.program_id(0)

    @pl.when(step == 0)
    def _():
        for h in range(HEADS):
            heads[pl.ds(h, ROWS, 8), :] = query_ref[:, h * HD : (h + 1) * HD].astype(F32)

    scale = LOG2E / math.sqrt(HD)
    token = iota((8, CTX), 1)
    for b in range(BLK):
        r = step * BLK + b
        wide = heads[pl.ds(pl.multiple_of(r * 8, 8), 8), :]
        query = wide.astype(BF)
        keys = cache_ref[b, :, 0:HD]
        raw = lax.dot_general(query, keys, (((1,), (1,)), ((), ())), preferred_element_type=F32)
        live = token < len_ref[r]
        raw = jnp.where(live, raw * scale, NEG)
        top = jnp.max(raw, axis=1, keepdims=True)
        prob = jnp.where(live, jnp.exp2(raw - top), 0.0).astype(BF)
        total = jnp.sum(prob.astype(F32), axis=1, keepdims=True)
        mix = jnp.dot(prob, cache_ref[b, :, HD:], preferred_element_type=F32)
        mix_ref[b] = mix * (1.0 / total)
        lse_ref[b] = jnp.broadcast_to(top * LN2 + jnp.log(total), (8, HD))
        new = jnp.sum(wide * new_ref[b], axis=1, keepdims=True) * (1.0 / math.sqrt(HD))
        score_ref[b] = jnp.broadcast_to(new, (8, HD))


def resident(lens, query, new_key, kv_cache):
    tile = pl.BlockSpec((BLK, 8, HD), lambda i: (i, 0, 0))
    shape = jax.ShapeDtypeStruct((ROWS, 8, HD), F32)
    return pl.pallas_call(
        resident_kernel,
        grid=(ROWS // BLK,),
        out_shape=(shape, shape, shape),
        in_specs=[
            SM,
            pl.BlockSpec((ROWS, HEADS * HD), lambda i: (0, 0)),
            pl.BlockSpec((BLK, 1, HD), lambda i: (i, 0, 0)),
            pl.BlockSpec((BLK, CTX, 2 * HD), lambda i: (i, 0, 0)),
        ],
        out_specs=(tile, tile, tile),
        scratch_shapes=[pltpu.VMEM((ROWS * 8, HD), F32)],
        compiler_params=params(16),
        cost_estimate=cost(4 * ROWS * 8 * CTX * HD, 9 << 20),
        name="resident_attention",
    )(lens, query, new_key, kv_cache)


def mix_kernel(
    owner_ref, pos_ref, recv_ref, conv_ref, x_ref, weight_ref, bias_ref, proj_ref,
    mixed_ref, window_ref, part_ref, send_ref,
):
    sub = iota((ROWS, 256), 0)
    lane = iota((ROWS, 256), 1)
    source = jnp.full((ROWS, 256), -1, I32)
    for r in range(ROWS):
        source = jnp.where(sub == r, source_of(owner_ref, pos_ref, r), source)
    base = jnp.where(source >= 0, source * 8, -8)
    pick = jnp.concatenate([(lane == base + k).astype(F32) for k in range(6)], axis=0).astype(BF)
    recv = recv_ref[...].reshape(256, HALF)
    prev = jnp.dot(pick, recv, preferred_element_type=F32)
    came = source[:, 0:1] >= 0
    x = x_ref[...]
    total = x.astype(F32) * weight_ref[3:4, :].astype(F32)
    window_ref[2] = x
    for j in range(3):
        here = jnp.concatenate(
            [prev[64 * j : 64 * j + 32], prev[64 * j + 32 : 64 * j + 64]], axis=1
        )
        tap = jnp.where(came, here, conv_ref[j].astype(F32))
        if j > 0:
            window_ref[j - 1] = tap.astype(BF)
        total += tap * weight_ref[j : j + 1, :].astype(F32)
    total += bias_ref[...]
    mixed = (total / (1.0 + jnp.exp(-total))).astype(BF)
    mixed_ref[...] = mixed
    part = lax.dot_general(
        mixed, proj_ref[...], (((1,), (1,)), ((), ())), preferred_element_type=F32
    )
    part_ref[...] = part
    send_ref[...] = part.astype(BF)


def mix(owner, pos, recv, conv_state, x_in, weight, bias, proj_t):
    wide = proj_t.shape[0]
    return pl.pallas_call(
        mix_kernel,
        out_shape=(
            jax.ShapeDtypeStruct((ROWS, EC), BF),
            jax.ShapeDtypeStruct((3, ROWS, EC), BF),
            jax.ShapeDtypeStruct((ROWS, wide), F32),
            jax.ShapeDtypeStruct((ROWS, wide), BF),
        ),
        in_specs=[SM, SM] + [VM] * 6,
        out_specs=(VM, VM, VM, VM),
        compiler_params=params(16),
        cost_estimate=cost(2 * ROWS * EC * wide, 4 << 20),
        name="mix_input",
    )(owner, pos, recv, conv_state, x_in, weight, bias, proj_t)


def step_kernel(*refs):
    part_ref = refs[0]
    others = refs[1:8]
    gain_ref, tail_gain_ref, proj_ref, bias_ref, mixed_ref, dt_ref, drive_ref, tail_ref = refs[8:]
    proj = part_ref[...]
    for other in others:
        proj += other[...].astype(F32)
    low = proj[:, 0:RANK]
    mean = jnp.sum(low * low, axis=1, keepdims=True) * (1.0 / RANK)
    normed = (low * lax.rsqrt(mean + 1e-6) * gain_ref[...]).astype(BF)
    dt = jnp.dot(normed, proj_ref[...], preferred_element_type=F32) + bias_ref[...]
    dt = jnp.maximum(dt, 0.0) + jnp.log1p(jnp.exp(-jnp.abs(dt)))
    dt_ref[...] = dt
    drive_ref[...] = dt * mixed_ref[...].astype(F32)
    tail = proj[:, RANK : RANK + 2 * NS]
    square = tail * tail
    front = iota((ROWS, 2 * NS), 1) < NS
    mean_b = jnp.sum(jnp.where(front, square, 0.0), axis=1, keepdims=True) * (1.0 / NS)
    mean_c = jnp.sum(jnp.where(front, 0.0, square), axis=1, keepdims=True) * (1.0 / NS)
    scale = lax.rsqrt(jnp.where(front, mean_b, mean_c) + 1e-6)
    tail_ref[...] = (tail * scale * tail_gain_ref[...]).astype(BF).astype(F32)


def step_size(part, others, gain, tail_gain, proj, bias, mixed):
    return pl.pallas_call(
        step_kernel,
        out_shape=(
            jax.ShapeDtypeStruct((ROWS, EC), F32),
            jax.ShapeDtypeStruct((ROWS, EC), F32),
            jax.ShapeDtypeStruct((ROWS, 2 * NS), F32),
        ),
        in_specs=[VM] * 13,
        out_specs=(VM, VM, VM),
        compiler_params=params(16),
        cost_estimate=cost(2 * ROWS * EC * RANK, 3 << 20),
        name="step_size",
    )(part, *others, gain, tail_gain, proj, bias, mixed)


GROUP = 8


def state_kernel(
    owner_ref, pos_ref, recv_ref, state_ref, dt_ref, drive_ref, tail_ref, decay_ref, skip_ref,
    z_ref, mixed_ref, new_ref, out_ref, local, prev, made, read, in_sems, out_sems,
):
    def fetch(r):
        return pltpu.make_async_copy(state_ref.at[r], local.at[r], in_sems.at[r])

    def store(i):
        rows = pl.ds(pl.multiple_of(i * GROUP, GROUP), GROUP)
        return pltpu.make_async_copy(made.at[i], new_ref.at[rows], out_sems.at[i])

    def begin(r, carry):
        @pl.when(owner_ref[r] < 0)
        def _():
            fetch(r).start()

        return carry

    lax.fori_loop(0, ROWS, begin, 0)

    def body(i, carry):
        for b in range(GROUP):
            r = i * GROUP + b
            source = source_of(owner_ref, pos_ref, r)

            @pl.when(source >= 0)
            def _():
                prev[b] = recv_ref[jnp.maximum(source, 0)].astype(F32)

            @pl.when(source < 0)
            def _():
                fetch(r).wait()
                prev[b] = local[r]

        rows = pl.ds(pl.multiple_of(i * GROUP, GROUP), GROUP)

        def column(c, inner):
            cols = pl.ds(pl.multiple_of(c * 128, 128), 128)
            dt = dt_ref[rows, cols]
            drive = drive_ref[rows, cols]
            decay = decay_ref[:, cols]
            sums = []
            for b in range(GROUP):
                r = i * GROUP + b
                inject = tail_ref[r, 0:NS, :]
                read_out = tail_ref[r, NS:, :]
                keep = jnp.exp(-dt[b : b + 1, :] * decay)
                new = keep * prev[b, :, cols] + drive[b : b + 1, :] * inject
                made[i, b, :, cols] = new
                sums.append(jnp.sum(new * read_out, axis=0, keepdims=True))
            read[rows, cols] = jnp.concatenate(sums, axis=0)
            return inner

        lax.fori_loop(0, EC // 128, column, 0)
        store(i).start()
        return carry

    lax.fori_loop(0, ROWS // GROUP, body, 0)
    z = z_ref[...].astype(F32)
    gate = z / (1.0 + jnp.exp(-z))
    mixed = mixed_ref[...].astype(F32)
    out_ref[...] = ((read[...] + skip_ref[...] * mixed) * gate).astype(BF)
    for i in range(ROWS // GROUP):
        store(i).wait()


def update_state(owner, pos, recv, state, dt, drive, tail, decay, skip, z, mixed):
    return pl.pallas_call(
        state_kernel,
        out_shape=(
            jax.ShapeDtypeStruct((ROWS, NS, EC), F32),
            jax.ShapeDtypeStruct((ROWS, EC), BF),
        ),
        in_specs=[SM, SM, VM, HB] + [VM] * 7,
        out_specs=(HB, VM),
        scratch_shapes=[
            pltpu.VMEM((ROWS, NS, EC), F32),
            pltpu.VMEM((GROUP, NS, EC), F32),
            pltpu.VMEM((ROWS // GROUP, GROUP, NS, EC), F32),
            pltpu.VMEM((ROWS, EC), F32),
            pltpu.SemaphoreType.DMA((ROWS,)),
            pltpu.SemaphoreType.DMA((ROWS // GROUP,)),
        ],
        compiler_params=params(24),
        cost_estimate=cost(16 << 20, 10 << 20),
        name="update_state",
    )(owner, pos, recv, state, dt, drive, tail, decay, skip, z, mixed)


def finish_kernel(
    owner_ref, pos_ref, recv_ref, mix_ref, lse_ref, score_ref, value_ref, out_ref, made, part
):
    for r in range(ROWS):
        source = source_of(owner_ref, pos_ref, r)
        tile = recv_ref[jnp.maximum(source, 0)].astype(F32)
        there = tile[8:16, 0:1] + tile[8:16, 32:33] + tile[8:16, 64:65]
        came = source >= 0
        lse = jnp.where(came, there, lse_ref[r])
        mix = jnp.where(came, tile[0:8, :], mix_ref[r])
        score = score_ref[r]
        peak = jnp.maximum(lse, score)
        old = jnp.exp(lse - peak)
        new = jnp.exp(score - peak)
        value = value_ref[r]
        made[8 * r : 8 * r + 8, :] = (mix * old + new * value) / (old + new)
    for h in range(HEADS):
        out_ref[:, h * HD : (h + 1) * HD] = made[pl.ds(h, ROWS, 8), :].astype(BF)


def finish(owner, pos, recv, mix, lse, score, value):
    return pl.pallas_call(
        finish_kernel,
        out_shape=jax.ShapeDtypeStruct((ROWS, HEADS * HD), BF),
        in_specs=[SM, SM] + [VM] * 5,
        out_specs=VM,
        scratch_shapes=[pltpu.VMEM((ROWS * 8, HD), F32), pltpu.VMEM((8, HD), F32)],
        compiler_params=params(16),
        cost_estimate=cost(1 << 16, 1 << 19),
        name="join_new_token",
    )(owner, pos, recv, mix, lse, score, value)


def swap(values):
    return lax.all_to_all(values, "rep", split_axis=0, concat_axis=0, tiled=True)


def shards(
    x_in, z_gate, conv_state, conv_pool, ssm_state, ssm_pool, conv_weight, conv_bias, x_proj,
    dt_gain, b_gain, c_gain, dt_proj, dt_bias, decay_rate, skip, query, new_kv, kv_cache, kv_pool,
    ctx_len, row_owner, row_pos, swap_slot, swap_lens, swap_pages,
):
    slots = swap_slot.transpose(0, 2, 1)
    first = swap(pack(slots, row_owner, row_pos, conv_pool.transpose(1, 0, 2), query))
    states = gather_states(slots, ssm_pool)
    second = swap(states.reshape(PEERS, CAP, NS, EC)).reshape(ENT, NS, EC)

    new_key = new_kv[:, None, 0:HD].astype(F32)
    new_value = new_kv[:, None, HD:].astype(F32)
    mix_here, lse_here, score = resident(ctx_len, query, new_key, kv_cache)
    pages = jnp.tile(swap_pages[0].reshape(ENT, CTX // PAGE).T, (1, 4))
    lens = jnp.tile(swap_lens[0].reshape(1, ENT), (1, 4))
    weight, vt = weigh(pages, lens, kv_pool)
    served = serve(first, kv_pool, weight, vt)
    third = swap(served).reshape(ENT, 16, HD)

    mixed, window, part, send = mix(
        row_owner, row_pos, first, conv_state.transpose(1, 0, 2), x_in, conv_weight,
        conv_bias.reshape(1, EC), x_proj.T,
    )
    tp = lax.axis_size("tp")
    others = [
        lax.ppermute(send, "tp", [(i, (i + s) % tp) for i in range(tp)]) for s in range(1, tp)
    ]
    dt, drive, tail = step_size(
        part, others, dt_gain.reshape(1, RANK), jnp.concatenate([b_gain, c_gain]).reshape(1, 2 * NS),
        dt_proj, dt_bias.reshape(1, EC), mixed,
    )
    tail = jnp.broadcast_to(tail[:, :, None], (ROWS, 2 * NS, 128))
    new_ssm, mamba_out = update_state(
        row_owner, row_pos, second, ssm_state, dt, drive, tail, decay_rate, skip.reshape(1, EC),
        z_gate, mixed,
    )
    attn_out = finish(row_owner, row_pos, third, mix_here, lse_here, score, new_value)
    return (mamba_out, attn_out, new_ssm, window.transpose(1, 0, 2))


def solution(mesh):
    in_specs = (
        P("rep", "tp"), P("rep", "tp"), P("rep", None, "tp"), P("rep", None, "tp"),
        P("rep", None, "tp"), P("rep", None, "tp"), P(None, "tp"), P("tp"), P("tp", None),
        P(), P(), P(), P(None, "tp"), P("tp"), P(None, "tp"), P("tp"), P("rep", "tp"),
        P("rep", "tp"), P("rep", None, "tp"), P("rep", None, "tp"), P("rep"), P("rep"), P("rep"),
        P("rep", None, None), P("rep", None, None), P("rep", None, None, None),
    )
    out_specs = (P("rep", "tp"), P("rep", "tp"), P("rep", None, "tp"), P("rep", None, "tp"))
    return jax.shard_map(shards, mesh=mesh, in_specs=in_specs, out_specs=out_specs, check_vma=False)
```

```python
import functools
import math

import jax
import jax.numpy as jnp
from jax import lax
from jax.experimental import pallas as pl
from jax.experimental.pallas import tpu as pltpu
from jax.sharding import PartitionSpec as P

BF = jnp.bfloat16
F32 = jnp.float32
I32 = jnp.int32
PEERS = 16
CAP = 2
LAST = 15
ENT = PEERS * CAP
ROWS = 32
EC = 2048
HALF = EC // 2
NS = 16
RANK = 512
HEADS = 8
HD = 128
CTX = 512
PAGE = 16
POOL = 256
TOK = POOL * PAGE
CHUNK = 256
LOG2E = 1.4426950408889634
LN2 = 0.6931471805599453
NEG = -1e30

VM = pl.BlockSpec(memory_space=pltpu.VMEM)
SM = pl.BlockSpec(memory_space=pltpu.SMEM)
AN = pl.BlockSpec(memory_space=pl.ANY)
HB = pl.BlockSpec(memory_space=pltpu.HBM)
WIDE = EC + HD
BIAS = math.sqrt(HD) / LOG2E


def iota(shape, dim):
    return lax.broadcasted_iota(I32, shape, dim)


def params(mib):
    return pltpu.CompilerParams(vmem_limit_bytes=mib * 1024 * 1024)


ALONE = pltpu.CompilerParams(vmem_limit_bytes=65716224)


def cost(flops, byts):
    return pl.CostEstimate(flops=flops, bytes_accessed=byts, transcendentals=0)


def pack_kernel(
    slot_hbm, owner_hbm, pos_hbm, conv_ref, query_ref, out_ref,
    stack, made, inverse, slot_ref, owner_ref, pos_ref, sems,
):
    copies = [
        pltpu.make_async_copy(slot_hbm, slot_ref, sems.at[0]),
        pltpu.make_async_copy(owner_hbm, owner_ref, sems.at[1]),
        pltpu.make_async_copy(pos_hbm, pos_ref, sems.at[2]),
        pltpu.make_async_copy(query_ref, stack.at[192:224], sems.at[3]),
    ]
    for k in range(6):
        j, h = k // 2, k % 2
        copies.append(
            pltpu.make_async_copy(
                conv_ref.at[j, :, h * HALF : (h + 1) * HALF],
                stack.at[32 * k : 32 * k + 32],
                sems.at[4 + k],
            )
        )
    for copy in copies:
        copy.start()
    stack[224:256, :] = jnp.zeros((32, HALF), BF)
    for e in range(ENT):
        inverse[e] = -1
    for copy in copies[:3]:
        copy.wait()
    for r in range(ROWS):
        owner = owner_ref[r]

        @pl.when(owner >= 0)
        def _():
            inverse[(LAST - owner) * CAP + pos_ref[r]] = 192 + r

    lane = iota((8, 256), 1)
    part = iota((8, 256), 0)
    tiles = []
    for e in range(ENT):
        slot = slot_ref[0, e % CAP, LAST - e // CAP]
        want = jnp.where(part < 6, 32 * part + slot, jnp.where(part == 6, inverse[e], -1))
        tiles.append((lane == want).astype(F32))
    pick = jnp.concatenate(tiles, axis=0).astype(BF)
    for copy in copies[3:]:
        copy.wait()
    gone = []
    for k in range(4):
        packed = jnp.dot(pick[64 * k : 64 * k + 64], stack[...], preferred_element_type=F32)
        made[4 * k : 4 * k + 4] = packed.astype(BF).reshape(4, 16, HALF)
        part = slice(4 * k, 4 * k + 4)
        gone.append(pltpu.make_async_copy(made.at[part], out_ref.at[part], sems.at[k]))
        gone[k].start()
    for copy in gone:
        copy.wait()


def pack(slots, owner, pos, conv_pool, query):
    return pl.pallas_call(
        pack_kernel,
        out_shape=jax.ShapeDtypeStruct((PEERS, 16, HALF), BF),
        in_specs=[HB] * 5,
        out_specs=HB,
        scratch_shapes=[
            pltpu.VMEM((256, HALF), BF),
            pltpu.VMEM((PEERS, 16, HALF), BF),
            pltpu.SMEM((ENT,), I32),
            pltpu.SMEM((1, CAP, PEERS), I32),
            pltpu.SMEM((ROWS,), I32),
            pltpu.SMEM((ROWS,), I32),
            pltpu.SemaphoreType.DMA((10,)),
        ],
        compiler_params=ALONE,
        cost_estimate=cost(2 * 256 * 256 * HALF, 1 << 20),
        name="pack_first",
    )(slots, owner, pos, conv_pool, query)


def prepare_kernel(
    slot_hbm, pages_hbm, lens_hbm, ssm_ref, states_ref, bias_ref, rest_ref,
    slot_ref, pages_ref, lens_ref, states, packed, sems, in_sems, out_sems,
):
    first = pltpu.make_async_copy(slot_hbm, slot_ref, sems.at[0])
    first.start()
    lists = [
        pltpu.make_async_copy(pages_hbm, pages_ref, sems.at[1]),
        pltpu.make_async_copy(lens_hbm, lens_ref, sems.at[2]),
    ]
    for copy in lists:
        copy.start()
    first.wait()

    def fetch(k):
        return pltpu.make_async_copy(
            ssm_ref.at[8 * k : 8 * k + 8], states.at[8 * k : 8 * k + 8], in_sems.at[k]
        )

    def give(k):
        return pltpu.make_async_copy(
            packed.at[8 * k : 8 * k + 8], states_ref.at[8 * k : 8 * k + 8, :, 0:EC], out_sems.at[k]
        )

    for k in range(4):
        fetch(k).start()
    for copy in lists:
        copy.wait()

    full = jnp.zeros((1, 128), F32)
    rest = jnp.zeros((1, 128), F32)
    pages = jnp.zeros((CTX // PAGE, 128), F32)
    for place in range(CAP):
        want = iota((PEERS, 128), 1) % ENT == (LAST - iota((PEERS, 128), 0)) * CAP + place
        want = want.astype(F32)
        lens = lens_ref[0, place : place + 1, :]
        count = lens // PAGE
        full += jnp.dot(count.astype(F32), want, preferred_element_type=F32)
        rest += jnp.dot((lens - count * PAGE).astype(F32), want, preferred_element_type=F32)
        pages += lax.dot_general(
            pages_ref[0, :, place, :].astype(F32), want, (((0,), (0,)), ((), ())),
            preferred_element_type=F32,
        )
    page_id = iota((POOL, 128), 0).astype(F32)
    total = jnp.zeros((POOL, 128), F32)
    last = jnp.full((1, 128), -1.0, F32)
    for j in range(CTX // PAGE):
        page = pages[j : j + 1, :]
        total += jnp.where(page_id == jnp.where(full > j, page, -1.0), 1.0, 0.0)
        last = jnp.where(full == j, page, last)

    def bias(count):
        return jnp.where(count > 0.0, jnp.log2(jnp.maximum(count, 1.0)) * BIAS, NEG)

    bias_ref[0] = bias(total)
    bias_ref[1] = bias(total + jnp.where(page_id == last, 1.0, 0.0))
    rest_ref[...] = rest
    for k in range(4):
        fetch(k).wait()
    for k in range(4):
        for e in range(8 * k, 8 * k + 8):
            packed[e] = states[slot_ref[0, e % CAP, LAST - e // CAP]].astype(BF)
        give(k).start()
    for k in range(4):
        give(k).wait()


def prepare(slots, pages, lens, ssm_pool):
    return pl.pallas_call(
        prepare_kernel,
        out_shape=(
            jax.ShapeDtypeStruct((ENT, NS, WIDE), BF),
            jax.ShapeDtypeStruct((2, POOL, 128), F32),
            jax.ShapeDtypeStruct((1, 128), F32),
        ),
        in_specs=[HB] * 4,
        out_specs=(HB, VM, VM),
        scratch_shapes=[
            pltpu.SMEM((1, CAP, PEERS), I32),
            pltpu.VMEM((1, PEERS, CAP, CTX // PAGE), I32),
            pltpu.VMEM((1, CAP, PEERS), I32),
            pltpu.VMEM((ENT, NS, EC), F32),
            pltpu.VMEM((ENT, NS, EC), BF),
            pltpu.SemaphoreType.DMA((3,)),
            pltpu.SemaphoreType.DMA((4,)),
            pltpu.SemaphoreType.DMA((4,)),
        ],
        compiler_params=ALONE,
        cost_estimate=cost(1 << 20, 6 << 20),
        name="prepare_owner",
    )(slots, pages, lens, ssm_pool)


PARTS = 4


def serve_kernel(
    recv_hbm, bias_hbm, rest_hbm, pool_hbm, send_ref, out_ref, flag_ref,
    recv_ref, bias_ref, rest_ref, pool_ref, scores, back, slab, sems,
):
    loads = [
        pltpu.make_async_copy(recv_hbm, recv_ref, sems.at[0]),
        pltpu.make_async_copy(bias_hbm, bias_ref, sems.at[1]),
        pltpu.make_async_copy(rest_hbm, rest_ref, sems.at[2]),
    ]
    for k in range(PARTS):
        part = slice(k * POOL // PARTS, (k + 1) * POOL // PARTS)
        loads.append(pltpu.make_async_copy(pool_hbm.at[part], pool_ref.at[part], sems.at[3 + k]))
    for copy in loads:
        copy.start()
    lane = iota((ENT, 256), 1)
    pick = (lane == 8 * iota((ENT, 256), 0) + 6).astype(F32).astype(BF)
    loads[0].wait()
    recv = recv_ref[...].reshape(256, HALF)
    query = jnp.dot(pick, recv, preferred_element_type=F32).astype(BF)
    query = jnp.concatenate([query[:, h * HD : (h + 1) * HD] for h in range(HEADS)], axis=0)
    scale = LOG2E / math.sqrt(HD)
    pages = CHUNK // PAGE
    loads[1].wait()
    loads[2].wait()
    held = iota((PAGE, 128), 0).astype(F32) < rest_ref[...]

    top = jnp.full((8, 256), NEG, F32)
    for c in range(TOK // CHUNK):
        if c % (TOK // CHUNK // PARTS) == 0:
            loads[3 + c // (TOK // CHUNK // PARTS)].wait()
        keys = pool_ref[c * pages : (c + 1) * pages, :, 0:HD].reshape(CHUNK, HD)
        raw = lax.dot_general(keys, query, (((1,), (1,)), ((), ())), preferred_element_type=F32)
        bias = jnp.concatenate(
            [
                jnp.where(held, bias_ref[1, p : p + 1, :], bias_ref[0, p : p + 1, :])
                for p in range(c * pages, (c + 1) * pages)
            ],
            axis=0,
        )
        raw = raw + jnp.concatenate([bias, bias], axis=1)
        scores[c * CHUNK : (c + 1) * CHUNK, :] = raw
        top = jnp.maximum(top, jnp.max(raw.reshape(CHUNK // 8, 8, 256), axis=0))
    top = jnp.max(top, axis=0, keepdims=True)

    mix = jnp.zeros((HD, 256), F32)
    total = jnp.zeros((8, 256), F32)
    for c in range(TOK // CHUNK):
        raw = scores[c * CHUNK : (c + 1) * CHUNK, :]
        prob = jnp.exp2((raw - top) * scale).astype(BF)
        total += jnp.sum(prob.astype(F32).reshape(CHUNK // 8, 8, 256), axis=0)
        mix += lax.dot_general(
            pool_ref[c * pages : (c + 1) * pages, :, HD:].reshape(CHUNK, HD), prob,
            (((0,), (0,)), ((), ())), preferred_element_type=F32,
        )
    total = jnp.sum(total, axis=0, keepdims=True)
    lse = top * (1.0 / math.sqrt(HD)) + jnp.log(total)
    high = lse.astype(BF).astype(F32)
    mid = (lse - high).astype(BF).astype(F32)
    low = lse - high - mid
    row = iota((HD, 256), 0)
    pieces = jnp.where(row < 32, high, jnp.where(row < 64, mid, low)).T
    mix = (mix * (1.0 / total)).T
    for h in range(HEADS):
        back[pl.ds(h, ENT, 16), :] = mix[h * ENT : (h + 1) * ENT, :]
        back[pl.ds(8 + h, ENT, 16), :] = pieces[h * ENT : (h + 1) * ENT, :]
    slab[...] = back[...].astype(BF).reshape(ENT, 16, HD)
    copy = pltpu.make_async_copy(slab, out_ref.at[:, :, EC:WIDE], sems.at[0])
    copy.start()
    flag_ref[...] = top[:, 0:HD]
    copy.wait()


def serve(recv, bias, rest, kv_pool, send):
    return pl.pallas_call(
        serve_kernel,
        out_shape=(
            jax.ShapeDtypeStruct((ENT, NS, WIDE), BF),
            jax.ShapeDtypeStruct((1, HD), F32),
        ),
        in_specs=[HB] * 4 + [AN],
        out_specs=(AN, VM),
        input_output_aliases={4: 0},
        scratch_shapes=[
            pltpu.VMEM((PEERS, 16, HALF), BF),
            pltpu.VMEM((2, POOL, 128), F32),
            pltpu.VMEM((1, 128), F32),
            pltpu.VMEM((POOL, PAGE, 2 * HD), BF),
            pltpu.VMEM((TOK, 256), F32),
            pltpu.VMEM((ENT * 16, HD), F32),
            pltpu.VMEM((ENT, 16, HD), BF),
            pltpu.SemaphoreType.DMA((3 + PARTS,)),
        ],
        compiler_params=ALONE,
        cost_estimate=cost(4 * TOK * 256 * HD, 6 << 20),
        name="serve_pool",
    )(recv, bias, rest, kv_pool, send)


BLK = 8


def resident_kernel(
    flag_ref, len_ref, query_ref, new_ref, cache_ref, mix_ref, score_ref, heads
):
    step = pl.program_id(0)

    @pl.when(step == 0)
    def _():
        for h in range(HEADS):
            heads[pl.ds(h, ROWS, 8), :] = query_ref[:, h * HD : (h + 1) * HD].astype(F32)

    scale = LOG2E / math.sqrt(HD)
    rows = BLK * 8
    wide = heads[pl.ds(pl.multiple_of(step * rows, rows), rows), :]
    query = wide.astype(BF)
    raw = []
    lens = []
    for b in range(BLK):
        raw.append(
            lax.dot_general(
                query[8 * b : 8 * b + 8], cache_ref[b, :, 0:HD], (((1,), (1,)), ((), ())),
                preferred_element_type=F32,
            )
        )
        lens.append(jnp.full((8, CTX), len_ref[step * BLK + b], I32))
    raw = jnp.concatenate(raw, axis=0)
    live = iota((rows, CTX), 1) < jnp.concatenate(lens, axis=0)
    raw = jnp.where(live, raw * scale, NEG)
    top = jnp.max(raw, axis=1, keepdims=True)
    prob = jnp.exp2(raw - top).astype(BF)
    total = jnp.sum(prob.astype(F32), axis=1, keepdims=True)
    mix = jnp.concatenate(
        [
            jnp.dot(prob[8 * b : 8 * b + 8], cache_ref[b, :, HD:], preferred_element_type=F32)
            for b in range(BLK)
        ],
        axis=0,
    )
    new = new_ref[...].astype(F32)
    key = jnp.concatenate(
        [jnp.broadcast_to(new[b : b + 1, 0:HD], (8, HD)) for b in range(BLK)], axis=0
    )
    value = jnp.concatenate(
        [jnp.broadcast_to(new[b : b + 1, HD:], (8, HD)) for b in range(BLK)], axis=0
    )
    score = jnp.sum(wide * key, axis=1, keepdims=True) * scale
    peak = jnp.maximum(top, score)
    old = jnp.exp2(top - peak)
    add = jnp.exp2(score - peak)
    mix_ref[...] = (mix * old + add * value) / (total * old + add)
    score_ref[...] = jnp.broadcast_to(score * LN2, (rows, HD))


def resident(flag, lens, query, new_kv, kv_cache):
    tile = pl.BlockSpec((BLK * 8, HD), lambda i: (i, 0))
    shape = jax.ShapeDtypeStruct((ROWS * 8, HD), F32)
    return pl.pallas_call(
        resident_kernel,
        grid=(ROWS // BLK,),
        out_shape=(shape, shape),
        in_specs=[
            AN,
            SM,
            pl.BlockSpec((ROWS, HEADS * HD), lambda i: (0, 0)),
            pl.BlockSpec((BLK, 2 * HD), lambda i: (i, 0)),
            pl.BlockSpec((BLK, CTX, 2 * HD), lambda i: (i, 0, 0)),
        ],
        out_specs=(tile, tile),
        scratch_shapes=[pltpu.VMEM((ROWS * 8, HD), F32)],
        compiler_params=params(58),
        cost_estimate=cost(4 * ROWS * 8 * CTX * HD, 9 << 20),
        name="resident_attention",
    )(flag, lens, query, new_kv, kv_cache)


def mix_kernel(
    flag_ref, source_ref, recv_ref, conv_ref, x_ref, weight_ref, bias_ref, proj_ref,
    mixed_ref, window_ref, part_ref, send_ref,
):
    sub = iota((ROWS, 256), 0)
    lane = iota((ROWS, 256), 1)
    source = jnp.full((ROWS, 256), -1, I32)
    for r in range(ROWS):
        source = jnp.where(sub == r, source_ref[r], source)
    base = jnp.where(source >= 0, source * 8, -8)
    pick = jnp.concatenate([(lane == base + k).astype(F32) for k in range(6)], axis=0).astype(BF)
    recv = recv_ref[...].reshape(256, HALF)
    prev = jnp.dot(pick, recv, preferred_element_type=F32)
    came = source[:, 0:1] >= 0
    x = x_ref[...]
    total = x.astype(F32) * weight_ref[3:4, :].astype(F32)
    window_ref[2] = x
    for j in range(3):
        here = jnp.concatenate(
            [prev[64 * j : 64 * j + 32], prev[64 * j + 32 : 64 * j + 64]], axis=1
        )
        tap = jnp.where(came, here, conv_ref[j].astype(F32))
        if j > 0:
            window_ref[j - 1] = tap.astype(BF)
        total += tap * weight_ref[j : j + 1, :].astype(F32)
    total += bias_ref[...]
    mixed = (total / (1.0 + jnp.exp(-total))).astype(BF)
    mixed_ref[...] = mixed
    part = lax.dot_general(
        mixed, proj_ref[...], (((1,), (1,)), ((), ())), preferred_element_type=F32
    )
    part_ref[...] = part
    send_ref[...] = part.astype(BF)


def mix(flag, source, recv, conv_state, x_in, weight, bias, proj_t):
    wide = proj_t.shape[0]
    return pl.pallas_call(
        mix_kernel,
        out_shape=(
            jax.ShapeDtypeStruct((ROWS, EC), BF),
            jax.ShapeDtypeStruct((3, ROWS, EC), BF),
            jax.ShapeDtypeStruct((ROWS, wide), F32),
            jax.ShapeDtypeStruct((ROWS, wide), BF),
        ),
        in_specs=[AN, SM] + [VM] * 6,
        out_specs=(VM, VM, VM, VM),
        compiler_params=ALONE,
        cost_estimate=cost(2 * ROWS * EC * wide, 4 << 20),
        name="mix_input",
    )(flag, source, recv, conv_state, x_in, weight, bias, proj_t)


GROUP = 8


def advance(prev, dt, decay, drive, inject):
    return jnp.exp2(dt * decay) * prev + drive * inject


def step_kernel(*refs):
    source_ref, part_ref = refs[0:2]
    others = refs[2:9]
    (
        gain_ref, tail_gain_ref, proj_ref, bias_ref, mixed_ref, skip_ref, z_ref, decay_ref, state_ref,
        dt_ref, drive_ref, inject_ref, read_ref, gate_ref, base_ref, new_ref,
        local, made, flat, in_sems, out_sems,
    ) = refs[9:]

    def fetch(r):
        return pltpu.make_async_copy(state_ref.at[r], local.at[r], in_sems.at[r])

    def store(r):
        return pltpu.make_async_copy(made.at[r], new_ref.at[r], out_sems.at[r])

    for r in range(ROWS):

        @pl.when(source_ref[r] < 0)
        def _():
            fetch(r).start()

    proj = part_ref[...]
    for other in others:
        proj += other[...].astype(F32)
    low = proj[:, 0:RANK]
    mean = jnp.sum(low * low, axis=1, keepdims=True) * (1.0 / RANK)
    normed = (low * lax.rsqrt(mean + 1e-6) * gain_ref[...]).astype(BF)
    dt = jnp.dot(normed, proj_ref[...], preferred_element_type=F32) + bias_ref[...]
    dt = jnp.maximum(dt, 0.0) + jnp.log1p(jnp.exp(-jnp.abs(dt)))
    mixed = mixed_ref[...].astype(F32)
    drive = dt * mixed
    dt = dt * (-LOG2E)
    for r in range(ROWS):
        dt_ref[r] = dt[r : r + 1, :]
        drive_ref[r] = drive[r : r + 1, :]
    z = z_ref[...].astype(F32)
    gate = z / (1.0 + jnp.exp(-z))
    gate_ref[...] = gate
    base_ref[...] = skip_ref[...] * mixed * gate
    tail = proj[:, RANK : RANK + 2 * NS]
    square = tail * tail
    front = iota((ROWS, 2 * NS), 1) < NS
    mean_b = jnp.sum(jnp.where(front, square, 0.0), axis=1, keepdims=True) * (1.0 / NS)
    mean_c = jnp.sum(jnp.where(front, 0.0, square), axis=1, keepdims=True) * (1.0 / NS)
    scale = lax.rsqrt(jnp.where(front, mean_b, mean_c) + 1e-6)
    tail = (tail * scale * tail_gain_ref[...]).astype(BF)
    lane = iota((2 * NS, 128), 1)
    spread = (iota((2 * NS, 128), 0) == NS + lane % NS).astype(F32).astype(BF)
    read = jnp.dot(tail, spread, preferred_element_type=F32)
    own = iota((ROWS, 128), 1) // NS == iota((ROWS, 128), 0) % GROUP
    read_ref[...] = jnp.where(own, read, 0.0)
    many = (iota((ROWS * NS, ROWS), 0) // NS == iota((ROWS * NS, ROWS), 1)).astype(F32).astype(BF)
    each = jnp.dot(many, tail, preferred_element_type=F32)
    mine = iota((ROWS * NS, 2 * NS), 0) % NS == iota((ROWS * NS, 2 * NS), 1)
    each = jnp.where(mine, each, 0.0).astype(BF)
    inject = jnp.dot(each, jnp.ones((2 * NS, 128), BF), preferred_element_type=F32)
    inject_ref[...] = inject.reshape(ROWS, NS, 128)

    def body(i, carry):
        for b in range(GROUP):
            r = i * GROUP + b

            @pl.when(source_ref[r] < 0)
            def _():
                fetch(r).wait()
                inject = jnp.concatenate([inject_ref[r]] * 4, axis=1)
                for c in range(EC // 512):
                    cols = slice(c * 512, (c + 1) * 512)
                    new = advance(
                        local[r, :, cols], dt_ref[r, :, cols], decay_ref[:, cols],
                        drive_ref[r, :, cols], inject,
                    )
                    made[r, :, cols] = new
                    flat[b * NS : (b + 1) * NS, cols] = new.astype(BF)
                store(r).start()

            @pl.when(source_ref[r] >= 0)
            def _():
                flat[b * NS : (b + 1) * NS, :] = jnp.zeros((NS, EC), BF)

        rows = pl.ds(pl.multiple_of(i * GROUP, GROUP), GROUP)
        sums = jnp.dot(read_ref[rows, :].astype(BF), flat[...], preferred_element_type=F32)
        base_ref[rows, :] += sums * gate_ref[rows, :]
        return carry

    lax.fori_loop(0, ROWS // GROUP, body, 0)
    for r in range(ROWS):

        @pl.when(source_ref[r] < 0)
        def _():
            store(r).wait()


def step_size(source, part, others, *operands):
    return pl.pallas_call(
        step_kernel,
        out_shape=(
            jax.ShapeDtypeStruct((ROWS, 1, EC), F32),
            jax.ShapeDtypeStruct((ROWS, 1, EC), F32),
            jax.ShapeDtypeStruct((ROWS, NS, 128), F32),
            jax.ShapeDtypeStruct((ROWS, 128), F32),
            jax.ShapeDtypeStruct((ROWS, EC), F32),
            jax.ShapeDtypeStruct((ROWS, EC), F32),
            jax.ShapeDtypeStruct((ROWS, NS, EC), F32),
        ),
        in_specs=[SM] + [VM] * 16 + [HB],
        out_specs=(VM,) * 6 + (HB,),
        scratch_shapes=[
            pltpu.VMEM((ROWS, NS, EC), F32),
            pltpu.VMEM((ROWS, NS, EC), F32),
            pltpu.VMEM((GROUP * NS, EC), BF),
            pltpu.SemaphoreType.DMA((ROWS,)),
            pltpu.SemaphoreType.DMA((ROWS,)),
        ],
        compiler_params=params(56),
        cost_estimate=cost(2 * ROWS * EC * RANK, 12 << 20),
        name="step_and_resident",
    )(source, part, *others, *operands)


def tail_kernel(
    source_ref, recv_hbm, dt_hbm, drive_hbm, inject_hbm, read_hbm, decay_hbm,
    gate_hbm, base_hbm, mix_hbm, score_hbm, new_kv_hbm, kept_ref,
    new_ref, out_hbm, attn_hbm,
    dt_ref, drive_ref, inject_ref, read_ref, decay_ref, gate_ref, base_ref, mix_ref, score_ref,
    new_kv_ref, out_ref, attn_ref,
    came, made, flat, sums, other, pieces, sems, in_sems, out_sems,
):
    def fetch(k):
        part = slice(k * GROUP, (k + 1) * GROUP)
        return pltpu.make_async_copy(recv_hbm.at[part], came.at[part], in_sems.at[k])

    pairs = [
        (dt_hbm, dt_ref), (drive_hbm, drive_ref), (inject_hbm, inject_ref), (read_hbm, read_ref),
        (decay_hbm, decay_ref), (mix_hbm, mix_ref), (gate_hbm, gate_ref), (base_hbm, base_ref),
        (score_hbm, score_ref), (new_kv_hbm, new_kv_ref),
    ]
    loads = [pltpu.make_async_copy(a, b, sems.at[k]) for k, (a, b) in enumerate(pairs)]
    for copy in loads[:5]:
        copy.start()
    for k in range(ENT // GROUP):
        fetch(k).start()
    for copy in loads[5:]:
        copy.start()
    for copy in loads[:6]:
        copy.wait()
    for k in range(ENT // GROUP):
        fetch(k).wait()

    def store(r):
        return pltpu.make_async_copy(made.at[r], new_ref.at[r], out_sems.at[r])

    def store_all(i):
        rows = pl.ds(pl.multiple_of(i * GROUP, GROUP), GROUP)
        return pltpu.make_async_copy(made.at[rows], new_ref.at[rows], out_sems.at[i * GROUP])

    def leave(i, act):
        count = jnp.int32(0)
        for b in range(GROUP):
            count += jnp.where(source_ref[i * GROUP + b] >= 0, 1, 0)

        @pl.when(count == GROUP)
        def _():
            act(store_all(i))

        @pl.when(count < GROUP)
        def _():
            for b in range(GROUP):
                r = i * GROUP + b

                @pl.when(source_ref[r] >= 0)
                def _():
                    act(store(r))

    lane = iota((8, HD), 1)
    huge = jnp.where(lane < 32, -NEG, 0.0)

    def body(i, carry):
        for b in range(GROUP):
            r = i * GROUP + b
            source = source_ref[r]
            here = pl.ds(pl.multiple_of(8 * r, 8), 8)

            @pl.when(source >= 0)
            def _():
                tile = came[source, :, EC:WIDE].astype(F32)
                other[here, :] = tile[0:8, :]
                pieces[here, :] = tile[8:16, :]
                inject = jnp.concatenate([inject_ref[r]] * 4, axis=1)
                for c in range(EC // 512):
                    cols = slice(c * 512, (c + 1) * 512)
                    new = advance(
                        came[source, :, cols].astype(F32), dt_ref[r, :, cols],
                        decay_ref[:, cols], drive_ref[r, :, cols], inject,
                    )
                    made[r, :, cols] = new
                    flat[b * NS : (b + 1) * NS, cols] = new.astype(BF)

            @pl.when(source < 0)
            def _():
                other[here, :] = mix_ref[here, :]
                pieces[here, :] = huge
                flat[b * NS : (b + 1) * NS, :] = jnp.zeros((NS, EC), BF)

        leave(i, lambda copy: copy.start())
        rows = pl.ds(pl.multiple_of(i * GROUP, GROUP), GROUP)
        sums[rows, :] = jnp.dot(
            read_ref[rows, :].astype(BF), flat[...], preferred_element_type=F32
        )
        return carry

    lax.fori_loop(0, ROWS // GROUP, body, 0)
    for copy in loads[6:]:
        copy.wait()
    out_ref[...] = (sums[...] * gate_ref[...] + base_ref[...]).astype(BF)
    give_out = pltpu.make_async_copy(out_ref, out_hbm, sems.at[0])
    give_out.start()
    lse = pieces[:, 0:1] + pieces[:, 32:33] + pieces[:, 64:65]
    score = score_ref[...]
    peak = jnp.maximum(lse, score)
    old = jnp.exp(lse - peak)
    new = jnp.exp(score - peak)
    value = new_kv_ref[:, HD:].astype(F32)
    value = jnp.concatenate(
        [jnp.broadcast_to(value[r : r + 1, :], (8, HD)) for r in range(ROWS)], axis=0
    )
    pieces[...] = (other[...] * old + new * value) / (old + new)
    for h in range(HEADS):
        attn_ref[:, h * HD : (h + 1) * HD] = pieces[pl.ds(h, ROWS, 8), :].astype(BF)
    give_attn = pltpu.make_async_copy(attn_ref, attn_hbm, sems.at[1])
    give_attn.start()
    give_out.wait()
    give_attn.wait()
    for i in range(ROWS // GROUP):
        leave(i, lambda copy: copy.wait())


def tail(*operands):
    return pl.pallas_call(
        tail_kernel,
        out_shape=(
            jax.ShapeDtypeStruct((ROWS, NS, EC), F32),
            jax.ShapeDtypeStruct((ROWS, EC), BF),
            jax.ShapeDtypeStruct((ROWS, HEADS * HD), BF),
        ),
        in_specs=[SM] + [HB] * 11 + [AN],
        out_specs=(AN, HB, HB),
        input_output_aliases={12: 0},
        scratch_shapes=[
            pltpu.VMEM((ROWS, 1, EC), F32),
            pltpu.VMEM((ROWS, 1, EC), F32),
            pltpu.VMEM((ROWS, NS, 128), F32),
            pltpu.VMEM((ROWS, 128), F32),
            pltpu.VMEM((NS, EC), F32),
            pltpu.VMEM((ROWS, EC), F32),
            pltpu.VMEM((ROWS, EC), F32),
            pltpu.VMEM((ROWS * 8, HD), F32),
            pltpu.VMEM((ROWS * 8, HD), F32),
            pltpu.VMEM((ROWS, 2 * HD), BF),
            pltpu.VMEM((ROWS, EC), BF),
            pltpu.VMEM((ROWS, HEADS * HD), BF),
            pltpu.VMEM((ROWS, NS, WIDE), BF),
            pltpu.VMEM((ROWS, NS, EC), F32),
            pltpu.VMEM((GROUP * NS, EC), BF),
            pltpu.VMEM((ROWS, EC), F32),
            pltpu.VMEM((ROWS * 8, HD), F32),
            pltpu.VMEM((ROWS * 8, HD), F32),
            pltpu.SemaphoreType.DMA((10,)),
            pltpu.SemaphoreType.DMA((ENT // GROUP,)),
            pltpu.SemaphoreType.DMA((ROWS,)),
        ],
        compiler_params=ALONE,
        cost_estimate=cost(16 << 20, 8 << 20),
        name="update_and_join",
    )(*operands)


def swap(values):
    order = [[LAST - p for p in range(PEERS)]]
    return lax.all_to_all(
        values, "rep", split_axis=0, concat_axis=0, tiled=True, axis_index_groups=order
    )


def shards(
    x_in, z_gate, conv_state, conv_pool, ssm_state, ssm_pool, conv_weight, conv_bias, x_proj,
    dt_gain, b_gain, c_gain, dt_proj, dt_bias, decay_rate, skip, query, new_kv, kv_cache, kv_pool,
    ctx_len, row_owner, row_pos, swap_slot, swap_lens, swap_pages,
):
    slots = swap_slot.transpose(0, 2, 1)
    first = swap(pack(slots, row_owner, row_pos, conv_pool.transpose(1, 0, 2), query))
    source = jnp.where(row_owner >= 0, (LAST - row_owner) * CAP + row_pos, -1)
    states, bias, rest = prepare(slots, swap_pages, swap_lens.transpose(0, 2, 1), ssm_pool)
    states, flag = serve(first, bias, rest, kv_pool, states)
    second = swap(states.reshape(PEERS, CAP * NS, WIDE)).reshape(ENT, NS, WIDE)

    mixed, window, part, send = mix(
        flag, source, first, conv_state.transpose(1, 0, 2), x_in, conv_weight,
        conv_bias.reshape(1, EC), x_proj.T,
    )
    tp = lax.axis_size("tp")
    others = [
        lax.ppermute(send, "tp", [(i, (i + s) % tp) for i in range(tp)]) for s in range(1, tp)
    ]
    mix_here, score = resident(flag, ctx_len, query, new_kv, kv_cache)
    dt, drive, inject, read, gate, base, kept = step_size(
        source, part, others, dt_gain.reshape(1, RANK),
        jnp.concatenate([b_gain, c_gain]).reshape(1, 2 * NS), dt_proj, dt_bias.reshape(1, EC), mixed,
        skip.reshape(1, EC), z_gate, decay_rate, ssm_state,
    )
    new_ssm, mamba_out, attn_out = tail(
        source, second, dt, drive, inject, read, decay_rate, gate, base, mix_here, score, new_kv, kept
    )
    return (mamba_out, attn_out, new_ssm, window.transpose(1, 0, 2))


def solution(mesh):
    in_specs = (
        P("rep", "tp"), P("rep", "tp"), P("rep", None, "tp"), P("rep", None, "tp"),
        P("rep", None, "tp"), P("rep", None, "tp"), P(None, "tp"), P("tp"), P("tp", None),
        P(), P(), P(), P(None, "tp"), P("tp"), P(None, "tp"), P("tp"), P("rep", "tp"),
        P("rep", "tp"), P("rep", None, "tp"), P("rep", None, "tp"), P("rep"), P("rep"), P("rep"),
        P("rep", None, None), P("rep", None, None), P("rep", None, None, None),
    )
    out_specs = (P("rep", "tp"), P("rep", "tp"), P("rep", None, "tp"), P("rep", None, "tp"))
    return jax.shard_map(shards, mesh=mesh, in_specs=in_specs, out_specs=out_specs, check_vma=False)
```

```python
import functools
import math

import jax
import jax.numpy as jnp
from jax import lax
from jax.experimental import pallas as pl
from jax.experimental.pallas import tpu as pltpu
from jax.sharding import PartitionSpec as P

BF = jnp.bfloat16
F32 = jnp.float32
I32 = jnp.int32
PEERS = 16
CAP = 2
LAST = 15
ENT = PEERS * CAP
ROWS = 32
EC = 2048
HALF = EC // 2
NS = 16
RANK = 512
HEADS = 8
HD = 128
CTX = 512
PAGE = 16
POOL = 256
TOK = POOL * PAGE
CHUNK = 256
LOG2E = 1.4426950408889634
LN2 = 0.6931471805599453
NEG = -1e30

VM = pl.BlockSpec(memory_space=pltpu.VMEM)
SM = pl.BlockSpec(memory_space=pltpu.SMEM)
AN = pl.BlockSpec(memory_space=pl.ANY)
HB = pl.BlockSpec(memory_space=pltpu.HBM)
WIDE = EC + HD
BIAS = math.sqrt(HD) / LOG2E


def iota(shape, dim):
    return lax.broadcasted_iota(I32, shape, dim)


def params(mib):
    return pltpu.CompilerParams(vmem_limit_bytes=mib * 1024 * 1024)


ALONE = pltpu.CompilerParams(vmem_limit_bytes=65716224)


def cost(flops, byts):
    return pl.CostEstimate(flops=flops, bytes_accessed=byts, transcendentals=0)


def pack_kernel(
    slot_hbm, owner_hbm, pos_hbm, conv_ref, query_ref, out_ref,
    stack, made, inverse, slot_ref, owner_ref, pos_ref, sems,
):
    copies = [
        pltpu.make_async_copy(slot_hbm, slot_ref, sems.at[0]),
        pltpu.make_async_copy(owner_hbm, owner_ref, sems.at[1]),
        pltpu.make_async_copy(pos_hbm, pos_ref, sems.at[2]),
        pltpu.make_async_copy(query_ref, stack.at[192:224], sems.at[3]),
    ]
    for k in range(6):
        j, h = k // 2, k % 2
        copies.append(
            pltpu.make_async_copy(
                conv_ref.at[j, :, h * HALF : (h + 1) * HALF],
                stack.at[32 * k : 32 * k + 32],
                sems.at[4 + k],
            )
        )
    for copy in copies:
        copy.start()
    stack[224:256, :] = jnp.zeros((32, HALF), BF)
    for e in range(ENT):
        inverse[e] = -1
    for copy in copies[:3]:
        copy.wait()
    for r in range(ROWS):
        owner = owner_ref[r]

        @pl.when(owner >= 0)
        def _():
            inverse[owner * CAP + pos_ref[r]] = 192 + r

    lane = iota((8, 256), 1)
    part = iota((8, 256), 0)
    tiles = []
    for e in range(ENT):
        slot = slot_ref[0, e % CAP, e // CAP]
        want = jnp.where(part < 6, 32 * part + slot, jnp.where(part == 6, inverse[e], -1))
        tiles.append((lane == want).astype(F32))
    pick = jnp.concatenate(tiles, axis=0).astype(BF)
    for copy in copies[3:]:
        copy.wait()
    gone = []
    for k in range(4):
        packed = jnp.dot(pick[64 * k : 64 * k + 64], stack[...], preferred_element_type=F32)
        made[4 * k : 4 * k + 4] = packed.astype(BF).reshape(4, 16, HALF)
        part = slice(4 * k, 4 * k + 4)
        gone.append(pltpu.make_async_copy(made.at[part], out_ref.at[part], sems.at[k]))
        gone[k].start()
    for copy in gone:
        copy.wait()


def pack(slots, owner, pos, conv_pool, query):
    return pl.pallas_call(
        pack_kernel,
        out_shape=jax.ShapeDtypeStruct((PEERS, 16, HALF), BF),
        in_specs=[HB] * 5,
        out_specs=HB,
        scratch_shapes=[
            pltpu.VMEM((256, HALF), BF),
            pltpu.VMEM((PEERS, 16, HALF), BF),
            pltpu.SMEM((ENT,), I32),
            pltpu.SMEM((1, CAP, PEERS), I32),
            pltpu.SMEM((ROWS,), I32),
            pltpu.SMEM((ROWS,), I32),
            pltpu.SemaphoreType.DMA((10,)),
        ],
        compiler_params=ALONE,
        cost_estimate=cost(2 * 256 * 256 * HALF, 1 << 20),
        name="pack_first",
    )(slots, owner, pos, conv_pool, query)


def prepare_kernel(
    slot_hbm, owner_hbm, pos_hbm, pages_hbm, lens_hbm, ssm_ref,
    states_ref, bias_ref, rest_ref, source_ref, state_source_ref,
    slot_ref, owner_ref, pos_ref, pages_ref, lens_ref, states, packed, sems, in_sems, out_sems,
):
    first = [
        pltpu.make_async_copy(slot_hbm, slot_ref, sems.at[0]),
        pltpu.make_async_copy(owner_hbm, owner_ref, sems.at[3]),
        pltpu.make_async_copy(pos_hbm, pos_ref, sems.at[4]),
    ]
    for copy in first:
        copy.start()
    lists = [
        pltpu.make_async_copy(pages_hbm, pages_ref, sems.at[1]),
        pltpu.make_async_copy(lens_hbm, lens_ref, sems.at[2]),
    ]
    for copy in lists:
        copy.start()
    for copy in first:
        copy.wait()

    def fetch(k):
        return pltpu.make_async_copy(
            ssm_ref.at[8 * k : 8 * k + 8], states.at[8 * k : 8 * k + 8], in_sems.at[k]
        )

    def give(k):
        return pltpu.make_async_copy(
            packed.at[8 * k : 8 * k + 8], states_ref.at[8 * k : 8 * k + 8, :, 0:EC], out_sems.at[k]
        )

    for k in range(4):
        fetch(k).start()
    for r in range(ROWS):
        owner = owner_ref[r]
        resumed = owner >= 0
        pos = pos_ref[r]
        source_ref[r] = jnp.where(resumed, owner * CAP + pos, -1)
        state_source_ref[r] = jnp.where(resumed, (LAST - owner) * CAP + pos, -1)
    for copy in lists:
        copy.wait()

    full = jnp.zeros((1, 128), F32)
    rest = jnp.zeros((1, 128), F32)
    pages = jnp.zeros((CTX // PAGE, 128), F32)
    for place in range(CAP):
        want = iota((PEERS, 128), 1) % ENT == (LAST - iota((PEERS, 128), 0)) * CAP + place
        want = want.astype(F32)
        lens = lens_ref[0, place : place + 1, :]
        count = lens // PAGE
        full += jnp.dot(count.astype(F32), want, preferred_element_type=F32)
        rest += jnp.dot((lens - count * PAGE).astype(F32), want, preferred_element_type=F32)
        pages += lax.dot_general(
            pages_ref[0, :, place, :].astype(F32), want, (((0,), (0,)), ((), ())),
            preferred_element_type=F32,
        )
    page_id = iota((POOL, 128), 0).astype(F32)
    total = jnp.zeros((POOL, 128), F32)
    last = jnp.full((1, 128), -1.0, F32)
    for j in range(CTX // PAGE):
        page = pages[j : j + 1, :]
        total += jnp.where(page_id == jnp.where(full > j, page, -1.0), 1.0, 0.0)
        last = jnp.where(full == j, page, last)

    def bias(count):
        return jnp.where(count > 0.0, jnp.log2(jnp.maximum(count, 1.0)) * BIAS, NEG)

    bias_ref[0] = bias(total)
    bias_ref[1] = bias(total + jnp.where(page_id == last, 1.0, 0.0))
    rest_ref[...] = rest
    for k in range(4):
        fetch(k).wait()
    for k in range(4):
        for e in range(8 * k, 8 * k + 8):
            packed[e] = states[slot_ref[0, e % CAP, LAST - e // CAP]].astype(BF)
        give(k).start()
    for k in range(4):
        give(k).wait()


def prepare(slots, owner, pos, pages, lens, ssm_pool):
    return pl.pallas_call(
        prepare_kernel,
        out_shape=(
            jax.ShapeDtypeStruct((ENT, NS, WIDE), BF),
            jax.ShapeDtypeStruct((2, POOL, 128), F32),
            jax.ShapeDtypeStruct((1, 128), F32),
            jax.ShapeDtypeStruct((ROWS,), I32),
            jax.ShapeDtypeStruct((ROWS,), I32),
        ),
        in_specs=[HB] * 6,
        out_specs=(HB, VM, VM, SM, SM),
        scratch_shapes=[
            pltpu.SMEM((1, CAP, PEERS), I32),
            pltpu.SMEM((ROWS,), I32),
            pltpu.SMEM((ROWS,), I32),
            pltpu.VMEM((1, PEERS, CAP, CTX // PAGE), I32),
            pltpu.VMEM((1, CAP, PEERS), I32),
            pltpu.VMEM((ENT, NS, EC), F32),
            pltpu.VMEM((ENT, NS, EC), BF),
            pltpu.SemaphoreType.DMA((5,)),
            pltpu.SemaphoreType.DMA((4,)),
            pltpu.SemaphoreType.DMA((4,)),
        ],
        compiler_params=ALONE,
        cost_estimate=cost(1 << 20, 6 << 20),
        name="prepare_owner",
    )(slots, owner, pos, pages, lens, ssm_pool)


PARTS = 4


def serve_kernel(
    recv_hbm, bias_hbm, rest_hbm, pool_hbm, send_ref, out_ref,
    recv_ref, bias_ref, rest_ref, pool_ref, scores, back, slab, sems,
):
    loads = [
        pltpu.make_async_copy(recv_hbm, recv_ref, sems.at[0]),
        pltpu.make_async_copy(bias_hbm, bias_ref, sems.at[1]),
        pltpu.make_async_copy(rest_hbm, rest_ref, sems.at[2]),
    ]
    for k in range(PARTS):
        part = slice(k * POOL // PARTS, (k + 1) * POOL // PARTS)
        loads.append(pltpu.make_async_copy(pool_hbm.at[part], pool_ref.at[part], sems.at[3 + k]))
    for copy in loads:
        copy.start()
    lane = iota((ENT, 256), 1)
    entry = iota((ENT, 256), 0)
    entry = CAP * (LAST - entry // CAP) + entry % CAP
    pick = (lane == 8 * entry + 6).astype(F32).astype(BF)
    loads[0].wait()
    recv = recv_ref[...].reshape(256, HALF)
    query = jnp.dot(pick, recv, preferred_element_type=F32).astype(BF)
    query = jnp.concatenate([query[:, h * HD : (h + 1) * HD] for h in range(HEADS)], axis=0)
    scale = LOG2E / math.sqrt(HD)
    pages = CHUNK // PAGE
    loads[1].wait()
    loads[2].wait()
    held = iota((PAGE, 128), 0).astype(F32) < rest_ref[...]

    top = jnp.full((8, 256), NEG, F32)
    for c in range(TOK // CHUNK):
        if c % (TOK // CHUNK // PARTS) == 0:
            loads[3 + c // (TOK // CHUNK // PARTS)].wait()
        keys = pool_ref[c * pages : (c + 1) * pages, :, 0:HD].reshape(CHUNK, HD)
        raw = lax.dot_general(keys, query, (((1,), (1,)), ((), ())), preferred_element_type=F32)
        bias = jnp.concatenate(
            [
                jnp.where(held, bias_ref[1, p : p + 1, :], bias_ref[0, p : p + 1, :])
                for p in range(c * pages, (c + 1) * pages)
            ],
            axis=0,
        )
        raw = raw + jnp.concatenate([bias, bias], axis=1)
        scores[c * CHUNK : (c + 1) * CHUNK, :] = raw
        top = jnp.maximum(top, jnp.max(raw.reshape(CHUNK // 8, 8, 256), axis=0))
    top = jnp.max(top, axis=0, keepdims=True)

    mix = jnp.zeros((HD, 256), F32)
    total = jnp.zeros((8, 256), F32)
    for c in range(TOK // CHUNK):
        raw = scores[c * CHUNK : (c + 1) * CHUNK, :]
        prob = jnp.exp2((raw - top) * scale).astype(BF)
        total += jnp.sum(prob.astype(F32).reshape(CHUNK // 8, 8, 256), axis=0)
        mix += lax.dot_general(
            pool_ref[c * pages : (c + 1) * pages, :, HD:].reshape(CHUNK, HD), prob,
            (((0,), (0,)), ((), ())), preferred_element_type=F32,
        )
    total = jnp.sum(total, axis=0, keepdims=True)
    lse = top * (1.0 / math.sqrt(HD)) + jnp.log(total)
    high = lse.astype(BF).astype(F32)
    mid = (lse - high).astype(BF).astype(F32)
    low = lse - high - mid
    row = iota((HD, 256), 0)
    pieces = jnp.where(row < 32, high, jnp.where(row < 64, mid, low)).T
    mix = (mix * (1.0 / total)).T
    for h in range(HEADS):
        back[pl.ds(h, ENT, 16), :] = mix[h * ENT : (h + 1) * ENT, :]
        back[pl.ds(8 + h, ENT, 16), :] = pieces[h * ENT : (h + 1) * ENT, :]
    slab[...] = back[...].astype(BF).reshape(ENT, 16, HD)
    copy = pltpu.make_async_copy(slab, out_ref.at[:, :, EC:WIDE], sems.at[0])
    copy.start()
    copy.wait()


def serve(recv, bias, rest, kv_pool, send):
    return pl.pallas_call(
        serve_kernel,
        out_shape=jax.ShapeDtypeStruct((ENT, NS, WIDE), BF),
        in_specs=[HB] * 4 + [AN],
        out_specs=AN,
        input_output_aliases={4: 0},
        scratch_shapes=[
            pltpu.VMEM((PEERS, 16, HALF), BF),
            pltpu.VMEM((2, POOL, 128), F32),
            pltpu.VMEM((1, 128), F32),
            pltpu.VMEM((POOL, PAGE, 2 * HD), BF),
            pltpu.VMEM((TOK, 256), F32),
            pltpu.VMEM((ENT * 16, HD), F32),
            pltpu.VMEM((ENT, 16, HD), BF),
            pltpu.SemaphoreType.DMA((3 + PARTS,)),
        ],
        compiler_params=ALONE,
        cost_estimate=cost(4 * TOK * 256 * HD, 6 << 20),
        name="serve_pool",
    )(recv, bias, rest, kv_pool, send)


BLK = 8


def resident_kernel(
    after_ref, len_ref, query_ref, new_ref, cache_ref, mix_ref, score_ref, heads
):
    step = pl.program_id(0)

    @pl.when(step == 0)
    def _():
        for h in range(HEADS):
            heads[pl.ds(h, ROWS, 8), :] = query_ref[:, h * HD : (h + 1) * HD].astype(F32)

    scale = LOG2E / math.sqrt(HD)
    rows = BLK * 8
    wide = heads[pl.ds(pl.multiple_of(step * rows, rows), rows), :]
    query = wide.astype(BF)
    raw = []
    lens = []
    for b in range(BLK):
        raw.append(
            lax.dot_general(
                query[8 * b : 8 * b + 8], cache_ref[b, :, 0:HD], (((1,), (1,)), ((), ())),
                preferred_element_type=F32,
            )
        )
        lens.append(jnp.full((8, CTX), len_ref[step * BLK + b], I32))
    raw = jnp.concatenate(raw, axis=0)
    live = iota((rows, CTX), 1) < jnp.concatenate(lens, axis=0)
    raw = jnp.where(live, raw * scale, NEG)
    top = jnp.max(raw, axis=1, keepdims=True)
    prob = jnp.exp2(raw - top).astype(BF)
    total = jnp.sum(prob.astype(F32), axis=1, keepdims=True)
    mix = jnp.concatenate(
        [
            jnp.dot(prob[8 * b : 8 * b + 8], cache_ref[b, :, HD:], preferred_element_type=F32)
            for b in range(BLK)
        ],
        axis=0,
    )
    new = new_ref[...].astype(F32)
    key = jnp.concatenate(
        [jnp.broadcast_to(new[b : b + 1, 0:HD], (8, HD)) for b in range(BLK)], axis=0
    )
    value = jnp.concatenate(
        [jnp.broadcast_to(new[b : b + 1, HD:], (8, HD)) for b in range(BLK)], axis=0
    )
    score = jnp.sum(wide * key, axis=1, keepdims=True) * scale
    peak = jnp.maximum(top, score)
    old = jnp.exp2(top - peak)
    add = jnp.exp2(score - peak)
    mix_ref[...] = (mix * old + add * value) / (total * old + add)
    score_ref[...] = jnp.broadcast_to(score * LN2, (rows, HD))


def resident(after, lens, query, new_kv, kv_cache):
    tile = pl.BlockSpec((BLK * 8, HD), lambda i: (i, 0))
    shape = jax.ShapeDtypeStruct((ROWS * 8, HD), F32)
    return pl.pallas_call(
        resident_kernel,
        grid=(ROWS // BLK,),
        out_shape=(shape, shape),
        in_specs=[
            AN,
            SM,
            pl.BlockSpec((ROWS, HEADS * HD), lambda i: (0, 0)),
            pl.BlockSpec((BLK, 2 * HD), lambda i: (i, 0)),
            pl.BlockSpec((BLK, CTX, 2 * HD), lambda i: (i, 0, 0)),
        ],
        out_specs=(tile, tile),
        scratch_shapes=[pltpu.VMEM((ROWS * 8, HD), F32)],
        compiler_params=params(58),
        cost_estimate=cost(4 * ROWS * 8 * CTX * HD, 9 << 20),
        name="resident_attention",
    )(after, lens, query, new_kv, kv_cache)


def mix_kernel(
    after_ref, source_ref, recv_ref, conv_ref, x_ref, weight_ref, bias_ref, proj_ref,
    mixed_ref, window_ref, part_ref, send_ref,
):
    sub = iota((ROWS, 256), 0)
    lane = iota((ROWS, 256), 1)
    source = jnp.full((ROWS, 256), -1, I32)
    for r in range(ROWS):
        source = jnp.where(sub == r, source_ref[r], source)
    base = jnp.where(source >= 0, source * 8, -8)
    pick = jnp.concatenate([(lane == base + k).astype(F32) for k in range(6)], axis=0).astype(BF)
    recv = recv_ref[...].reshape(256, HALF)
    prev = jnp.dot(pick, recv, preferred_element_type=F32)
    came = source[:, 0:1] >= 0
    x = x_ref[...]
    total = x.astype(F32) * weight_ref[3:4, :].astype(F32)
    window_ref[2] = x
    for j in range(3):
        here = jnp.concatenate(
            [prev[64 * j : 64 * j + 32], prev[64 * j + 32 : 64 * j + 64]], axis=1
        )
        tap = jnp.where(came, here, conv_ref[j].astype(F32))
        if j > 0:
            window_ref[j - 1] = tap.astype(BF)
        total += tap * weight_ref[j : j + 1, :].astype(F32)
    total += bias_ref[...]
    mixed = (total / (1.0 + jnp.exp(-total))).astype(BF)
    mixed_ref[...] = mixed
    part = lax.dot_general(
        mixed, proj_ref[...], (((1,), (1,)), ((), ())), preferred_element_type=F32
    )
    part_ref[...] = part
    send_ref[...] = part.astype(BF)


def mix(after, source, recv, conv_state, x_in, weight, bias, proj_t):
    wide = proj_t.shape[0]
    return pl.pallas_call(
        mix_kernel,
        out_shape=(
            jax.ShapeDtypeStruct((ROWS, EC), BF),
            jax.ShapeDtypeStruct((3, ROWS, EC), BF),
            jax.ShapeDtypeStruct((ROWS, wide), F32),
            jax.ShapeDtypeStruct((ROWS, wide), BF),
        ),
        in_specs=[AN, SM] + [VM] * 6,
        out_specs=(VM, VM, VM, VM),
        compiler_params=ALONE,
        cost_estimate=cost(2 * ROWS * EC * wide, 4 << 20),
        name="mix_input",
    )(after, source, recv, conv_state, x_in, weight, bias, proj_t)


GROUP = 8


def advance(prev, dt, decay, drive, inject):
    return jnp.exp2(dt * decay) * prev + drive * inject


def step_kernel(*refs):
    source_ref, part_ref = refs[0:2]
    others = refs[2:9]
    (
        gain_ref, b_gain_ref, c_gain_ref, proj_ref, bias_ref, mixed_ref, skip_ref, z_ref, decay_ref, state_ref,
        dt_ref, drive_ref, inject_ref, read_ref, gate_ref, base_ref, new_ref,
        local, made, flat, in_sems, out_sems,
    ) = refs[9:]

    def fetch(r):
        return pltpu.make_async_copy(state_ref.at[r], local.at[r], in_sems.at[r])

    def store(r):
        return pltpu.make_async_copy(made.at[r], new_ref.at[r], out_sems.at[r])

    for r in range(ROWS):

        @pl.when(source_ref[r] < 0)
        def _():
            fetch(r).start()

    proj = part_ref[...]
    for other in others:
        proj += other[...].astype(F32)
    low = proj[:, 0:RANK]
    mean = jnp.sum(low * low, axis=1, keepdims=True) * (1.0 / RANK)
    normed = (low * lax.rsqrt(mean + 1e-6) * gain_ref[...]).astype(BF)
    dt = jnp.dot(normed, proj_ref[...], preferred_element_type=F32) + bias_ref[...]
    dt = jnp.maximum(dt, 0.0) + jnp.log1p(jnp.exp(-jnp.abs(dt)))
    mixed = mixed_ref[...].astype(F32)
    drive = dt * mixed
    dt = dt * (-LOG2E)
    for r in range(ROWS):
        dt_ref[r] = dt[r : r + 1, :]
        drive_ref[r] = drive[r : r + 1, :]
    z = z_ref[...].astype(F32)
    gate = z / (1.0 + jnp.exp(-z))
    gate_ref[...] = gate
    base_ref[...] = skip_ref[...] * mixed * gate
    tail = proj[:, RANK : RANK + 2 * NS]
    square = tail * tail
    front = iota((ROWS, 2 * NS), 1) < NS
    mean_b = jnp.sum(jnp.where(front, square, 0.0), axis=1, keepdims=True) * (1.0 / NS)
    mean_c = jnp.sum(jnp.where(front, 0.0, square), axis=1, keepdims=True) * (1.0 / NS)
    scale = lax.rsqrt(jnp.where(front, mean_b, mean_c) + 1e-6)
    tail_gain = jnp.concatenate([b_gain_ref[...], c_gain_ref[...]], axis=1)
    tail = (tail * scale * tail_gain).astype(BF)
    lane = iota((2 * NS, 128), 1)
    spread = (iota((2 * NS, 128), 0) == NS + lane % NS).astype(F32).astype(BF)
    read = jnp.dot(tail, spread, preferred_element_type=F32)
    own = iota((ROWS, 128), 1) // NS == iota((ROWS, 128), 0) % GROUP
    read_ref[...] = jnp.where(own, read, 0.0)
    many = (iota((ROWS * NS, ROWS), 0) // NS == iota((ROWS * NS, ROWS), 1)).astype(F32).astype(BF)
    each = jnp.dot(many, tail, preferred_element_type=F32)
    mine = iota((ROWS * NS, 2 * NS), 0) % NS == iota((ROWS * NS, 2 * NS), 1)
    each = jnp.where(mine, each, 0.0).astype(BF)
    inject = jnp.dot(each, jnp.ones((2 * NS, 128), BF), preferred_element_type=F32)
    inject_ref[...] = inject.reshape(ROWS, NS, 128)

    def body(i, carry):
        for b in range(GROUP):
            r = i * GROUP + b

            @pl.when(source_ref[r] < 0)
            def _():
                fetch(r).wait()
                inject = jnp.concatenate([inject_ref[r]] * 4, axis=1)
                for c in range(EC // 512):
                    cols = slice(c * 512, (c + 1) * 512)
                    new = advance(
                        local[r, :, cols], dt_ref[r, :, cols], decay_ref[:, cols],
                        drive_ref[r, :, cols], inject,
                    )
                    made[r, :, cols] = new
                    flat[b * NS : (b + 1) * NS, cols] = new.astype(BF)
                store(r).start()

            @pl.when(source_ref[r] >= 0)
            def _():
                flat[b * NS : (b + 1) * NS, :] = jnp.zeros((NS, EC), BF)

        rows = pl.ds(pl.multiple_of(i * GROUP, GROUP), GROUP)
        sums = jnp.dot(read_ref[rows, :].astype(BF), flat[...], preferred_element_type=F32)
        base_ref[rows, :] += sums * gate_ref[rows, :]
        return carry

    lax.fori_loop(0, ROWS // GROUP, body, 0)
    for r in range(ROWS):

        @pl.when(source_ref[r] < 0)
        def _():
            store(r).wait()


def step_size(source, part, others, *operands):
    return pl.pallas_call(
        step_kernel,
        out_shape=(
            jax.ShapeDtypeStruct((ROWS, 1, EC), F32),
            jax.ShapeDtypeStruct((ROWS, 1, EC), F32),
            jax.ShapeDtypeStruct((ROWS, NS, 128), F32),
            jax.ShapeDtypeStruct((ROWS, 128), F32),
            jax.ShapeDtypeStruct((ROWS, EC), F32),
            jax.ShapeDtypeStruct((ROWS, EC), F32),
            jax.ShapeDtypeStruct((ROWS, NS, EC), F32),
        ),
        in_specs=[SM] + [VM] * 17 + [HB],
        out_specs=(VM,) * 6 + (HB,),
        scratch_shapes=[
            pltpu.VMEM((ROWS, NS, EC), F32),
            pltpu.VMEM((ROWS, NS, EC), F32),
            pltpu.VMEM((GROUP * NS, EC), BF),
            pltpu.SemaphoreType.DMA((ROWS,)),
            pltpu.SemaphoreType.DMA((ROWS,)),
        ],
        compiler_params=params(56),
        cost_estimate=cost(2 * ROWS * EC * RANK, 12 << 20),
        name="step_and_resident",
    )(source, part, *others, *operands)


def tail_kernel(
    source_ref, came, dt_ref, drive_ref, inject_ref, read_ref, decay_ref,
    gate_ref, base_ref, mix_ref, score_ref, new_kv_ref, kept_ref,
    new_ref, out_hbm, attn_hbm,
    out_ref, attn_ref, made, flat, sums, other, pieces, sems, out_sems,
):
    def store(r):
        return pltpu.make_async_copy(made.at[r], new_ref.at[r], out_sems.at[r])

    def store_all(i):
        rows = pl.ds(pl.multiple_of(i * GROUP, GROUP), GROUP)
        return pltpu.make_async_copy(made.at[rows], new_ref.at[rows], out_sems.at[i * GROUP])

    def leave(i, act):
        count = jnp.int32(0)
        for b in range(GROUP):
            count += jnp.where(source_ref[i * GROUP + b] >= 0, 1, 0)

        @pl.when(count == GROUP)
        def _():
            act(store_all(i))

        @pl.when(count < GROUP)
        def _():
            for b in range(GROUP):
                r = i * GROUP + b

                @pl.when(source_ref[r] >= 0)
                def _():
                    act(store(r))

    lane = iota((8, HD), 1)
    huge = jnp.where(lane < 32, -NEG, 0.0)

    def body(i, carry):
        for b in range(GROUP):
            r = i * GROUP + b
            source = source_ref[r]
            here = pl.ds(pl.multiple_of(8 * r, 8), 8)

            @pl.when(source >= 0)
            def _():
                tile = came[source, :, EC:WIDE].astype(F32)
                other[here, :] = tile[0:8, :]
                pieces[here, :] = tile[8:16, :]
                inject = jnp.concatenate([inject_ref[r]] * 4, axis=1)
                for c in range(EC // 512):
                    cols = slice(c * 512, (c + 1) * 512)
                    new = advance(
                        came[source, :, cols].astype(F32), dt_ref[r, :, cols],
                        decay_ref[:, cols], drive_ref[r, :, cols], inject,
                    )
                    made[r, :, cols] = new
                    flat[b * NS : (b + 1) * NS, cols] = new.astype(BF)

            @pl.when(source < 0)
            def _():
                other[here, :] = mix_ref[here, :]
                pieces[here, :] = huge
                flat[b * NS : (b + 1) * NS, :] = jnp.zeros((NS, EC), BF)

        leave(i, lambda copy: copy.start())
        rows = pl.ds(pl.multiple_of(i * GROUP, GROUP), GROUP)
        sums[rows, :] = jnp.dot(
            read_ref[rows, :].astype(BF), flat[...], preferred_element_type=F32
        )
        return carry

    lax.fori_loop(0, ROWS // GROUP, body, 0)
    out_ref[...] = (sums[...] * gate_ref[...] + base_ref[...]).astype(BF)
    give_out = pltpu.make_async_copy(out_ref, out_hbm, sems.at[0])
    give_out.start()
    lse = pieces[:, 0:1] + pieces[:, 32:33] + pieces[:, 64:65]
    score = score_ref[...]
    peak = jnp.maximum(lse, score)
    old = jnp.exp(lse - peak)
    new = jnp.exp(score - peak)
    value = new_kv_ref[:, HD:].astype(F32)
    value = jnp.concatenate(
        [jnp.broadcast_to(value[r : r + 1, :], (8, HD)) for r in range(ROWS)], axis=0
    )
    pieces[...] = (other[...] * old + new * value) / (old + new)
    for h in range(HEADS):
        attn_ref[:, h * HD : (h + 1) * HD] = pieces[pl.ds(h, ROWS, 8), :].astype(BF)
    give_attn = pltpu.make_async_copy(attn_ref, attn_hbm, sems.at[1])
    give_attn.start()
    give_out.wait()
    give_attn.wait()
    for i in range(ROWS // GROUP):
        leave(i, lambda copy: copy.wait())


def tail(*operands):
    return pl.pallas_call(
        tail_kernel,
        out_shape=(
            jax.ShapeDtypeStruct((ROWS, NS, EC), F32),
            jax.ShapeDtypeStruct((ROWS, EC), BF),
            jax.ShapeDtypeStruct((ROWS, HEADS * HD), BF),
        ),
        in_specs=[SM] + [VM] * 11 + [AN],
        out_specs=(AN, HB, HB),
        input_output_aliases={12: 0},
        scratch_shapes=[
            pltpu.VMEM((ROWS, EC), BF),
            pltpu.VMEM((ROWS, HEADS * HD), BF),
            pltpu.VMEM((ROWS, NS, EC), F32),
            pltpu.VMEM((GROUP * NS, EC), BF),
            pltpu.VMEM((ROWS, EC), F32),
            pltpu.VMEM((ROWS * 8, HD), F32),
            pltpu.VMEM((ROWS * 8, HD), F32),
            pltpu.SemaphoreType.DMA((10,)),
            pltpu.SemaphoreType.DMA((ROWS,)),
        ],
        compiler_params=ALONE,
        cost_estimate=cost(16 << 20, 8 << 20),
        name="update_and_join",
    )(*operands)


def swap(values, order):
    return lax.all_to_all(
        values, "rep", split_axis=0, concat_axis=0, tiled=True, axis_index_groups=[order]
    )


def shards(
    x_in, z_gate, conv_state, conv_pool, ssm_state, ssm_pool, conv_weight, conv_bias, x_proj,
    dt_gain, b_gain, c_gain, dt_proj, dt_bias, decay_rate, skip, query, new_kv, kv_cache, kv_pool,
    ctx_len, row_owner, row_pos, swap_slot, swap_lens, swap_pages,
):
    slots = swap_slot.transpose(0, 2, 1)
    peers = list(range(PEERS))
    first = swap(pack(slots, row_owner, row_pos, conv_pool.transpose(1, 0, 2), query), peers)
    states, bias, rest, source, state_source = prepare(
        slots, row_owner, row_pos, swap_pages, swap_lens.transpose(0, 2, 1), ssm_pool
    )
    states = serve(first, bias, rest, kv_pool, states)
    second = swap(states.reshape(PEERS, CAP * NS, WIDE), peers[::-1]).reshape(ENT, NS, WIDE)

    mixed, window, part, send = mix(
        states, source, first, conv_state.transpose(1, 0, 2), x_in, conv_weight,
        conv_bias.reshape(1, EC), x_proj.T,
    )
    tp = lax.axis_size("tp")
    others = [
        lax.ppermute(send, "tp", [(i, (i + s) % tp) for i in range(tp)]) for s in range(1, tp)
    ]
    mix_here, score = resident(states, ctx_len, query, new_kv, kv_cache)
    dt, drive, inject, read, gate, base, kept = step_size(
        state_source, part, others, dt_gain.reshape(1, RANK),
        b_gain.reshape(1, NS), c_gain.reshape(1, NS), dt_proj, dt_bias.reshape(1, EC), mixed,
        skip.reshape(1, EC), z_gate, decay_rate, ssm_state,
    )
    new_ssm, mamba_out, attn_out = tail(
        state_source, second, dt, drive, inject, read, decay_rate, gate, base, mix_here, score, new_kv, kept
    )
    return (mamba_out, attn_out, new_ssm, window.transpose(1, 0, 2))


def solution(mesh):
    in_specs = (
        P("rep", "tp"), P("rep", "tp"), P("rep", None, "tp"), P("rep", None, "tp"),
        P("rep", None, "tp"), P("rep", None, "tp"), P(None, "tp"), P("tp"), P("tp", None),
        P(), P(), P(), P(None, "tp"), P("tp"), P(None, "tp"), P("tp"), P("rep", "tp"),
        P("rep", "tp"), P("rep", None, "tp"), P("rep", None, "tp"), P("rep"), P("rep"), P("rep"),
        P("rep", None, None), P("rep", None, None), P("rep", None, None, None),
    )
    out_specs = (P("rep", "tp"), P("rep", "tp"), P("rep", None, "tp"), P("rep", None, "tp"))
    return jax.shard_map(shards, mesh=mesh, in_specs=in_specs, out_specs=out_specs, check_vma=False)
```

```python
import functools
import math

import jax
import jax.numpy as jnp
from jax import lax
from jax.experimental import pallas as pl
from jax.experimental.pallas import tpu as pltpu
from jax.sharding import PartitionSpec as P

BF = jnp.bfloat16
F32 = jnp.float32
I32 = jnp.int32
PEERS = 16
CAP = 2
SIDE = 4
ENT = PEERS * CAP
ROWS = 32
EC = 2048
HALF = EC // 2
NS = 16
RANK = 512
HEADS = 8
HD = 128
CTX = 512
PAGE = 16
POOL = 256
TOK = POOL * PAGE
CHUNK = 256
LOG2E = 1.4426950408889634
LN2 = 0.6931471805599453
NEG = -1e30

VM = pl.BlockSpec(memory_space=pltpu.VMEM)
SM = pl.BlockSpec(memory_space=pltpu.SMEM)
AN = pl.BlockSpec(memory_space=pl.ANY)
HB = pl.BlockSpec(memory_space=pltpu.HBM)
WIDE = EC + HD
BIAS = math.sqrt(HD) / LOG2E


def iota(shape, dim):
    return lax.broadcasted_iota(I32, shape, dim)


def first_peer(chunk):
    return (chunk + PEERS - SIDE) % PEERS


def first_chunk(peer):
    return (peer + SIDE) % PEERS


def second_peer(chunk):
    return PEERS - 1 - SIDE * (chunk % SIDE) - chunk // SIDE


second_chunk = second_peer


def params(mib):
    return pltpu.CompilerParams(vmem_limit_bytes=mib * 1024 * 1024)


ALONE = pltpu.CompilerParams(vmem_limit_bytes=65716224)


def cost(flops, byts):
    return pl.CostEstimate(flops=flops, bytes_accessed=byts, transcendentals=0)


def pack_kernel(
    slot_hbm, owner_hbm, pos_hbm, conv_ref, query_ref, out_ref,
    stack, made, inverse, slot_ref, owner_ref, pos_ref, sems,
):
    copies = [
        pltpu.make_async_copy(slot_hbm, slot_ref, sems.at[0]),
        pltpu.make_async_copy(owner_hbm, owner_ref, sems.at[1]),
        pltpu.make_async_copy(pos_hbm, pos_ref, sems.at[2]),
        pltpu.make_async_copy(query_ref, stack.at[192:224], sems.at[3]),
    ]
    for k in range(6):
        j, h = k // 2, k % 2
        copies.append(
            pltpu.make_async_copy(
                conv_ref.at[j, :, h * HALF : (h + 1) * HALF],
                stack.at[32 * k : 32 * k + 32],
                sems.at[4 + k],
            )
        )
    for copy in copies:
        copy.start()
    stack[224:256, :] = jnp.zeros((32, HALF), BF)
    for e in range(ENT):
        inverse[e] = -1
    for copy in copies[:3]:
        copy.wait()
    for r in range(ROWS):
        owner = owner_ref[r]

        @pl.when(owner >= 0)
        def _():
            inverse[first_chunk(owner) * CAP + pos_ref[r]] = 192 + r

    lane = iota((8, 256), 1)
    part = iota((8, 256), 0)
    tiles = []
    for e in range(ENT):
        slot = slot_ref[0, e % CAP, first_peer(e // CAP)]
        want = jnp.where(part < 6, 32 * part + slot, jnp.where(part == 6, inverse[e], -1))
        tiles.append((lane == want).astype(F32))
    pick = jnp.concatenate(tiles, axis=0).astype(BF)
    for copy in copies[3:]:
        copy.wait()
    gone = []
    for k in range(4):
        packed = jnp.dot(pick[64 * k : 64 * k + 64], stack[...], preferred_element_type=F32)
        made[4 * k : 4 * k + 4] = packed.astype(BF).reshape(4, 16, HALF)
        part = slice(4 * k, 4 * k + 4)
        gone.append(pltpu.make_async_copy(made.at[part], out_ref.at[part], sems.at[k]))
        gone[k].start()
    for copy in gone:
        copy.wait()


def pack(slots, owner, pos, conv_pool, query):
    return pl.pallas_call(
        pack_kernel,
        out_shape=jax.ShapeDtypeStruct((PEERS, 16, HALF), BF),
        in_specs=[HB] * 5,
        out_specs=HB,
        scratch_shapes=[
            pltpu.VMEM((256, HALF), BF),
            pltpu.VMEM((PEERS, 16, HALF), BF),
            pltpu.SMEM((ENT,), I32),
            pltpu.SMEM((1, CAP, PEERS), I32),
            pltpu.SMEM((ROWS,), I32),
            pltpu.SMEM((ROWS,), I32),
            pltpu.SemaphoreType.DMA((10,)),
        ],
        compiler_params=ALONE,
        cost_estimate=cost(2 * 256 * 256 * HALF, 1 << 20),
        name="pack_first",
    )(slots, owner, pos, conv_pool, query)


def prepare_kernel(
    slot_hbm, owner_hbm, pos_hbm, pages_hbm, lens_hbm, ssm_ref,
    states_ref, bias_ref, rest_ref, source_ref, state_source_ref,
    slot_ref, owner_ref, pos_ref, pages_ref, lens_ref, states, packed, sems, in_sems, out_sems,
):
    first = [
        pltpu.make_async_copy(slot_hbm, slot_ref, sems.at[0]),
        pltpu.make_async_copy(owner_hbm, owner_ref, sems.at[3]),
        pltpu.make_async_copy(pos_hbm, pos_ref, sems.at[4]),
    ]
    for copy in first:
        copy.start()
    lists = [
        pltpu.make_async_copy(pages_hbm, pages_ref, sems.at[1]),
        pltpu.make_async_copy(lens_hbm, lens_ref, sems.at[2]),
    ]
    for copy in lists:
        copy.start()
    for copy in first:
        copy.wait()

    def fetch(k):
        return pltpu.make_async_copy(
            ssm_ref.at[8 * k : 8 * k + 8], states.at[8 * k : 8 * k + 8], in_sems.at[k]
        )

    def give(k):
        return pltpu.make_async_copy(
            packed.at[8 * k : 8 * k + 8], states_ref.at[8 * k : 8 * k + 8, :, 0:EC], out_sems.at[k]
        )

    for k in range(4):
        fetch(k).start()
    for r in range(ROWS):
        resumed = owner_ref[r] >= 0
        owner = jnp.maximum(owner_ref[r], 0)
        pos = pos_ref[r]
        source_ref[r] = jnp.where(resumed, first_chunk(owner) * CAP + pos, -1)
        state_source_ref[r] = jnp.where(resumed, second_chunk(owner) * CAP + pos, -1)
    for copy in lists:
        copy.wait()

    full = jnp.zeros((1, 128), F32)
    rest = jnp.zeros((1, 128), F32)
    pages = jnp.zeros((CTX // PAGE, 128), F32)
    for place in range(CAP):
        want = iota((PEERS, 128), 1) % ENT == second_chunk(iota((PEERS, 128), 0)) * CAP + place
        want = want.astype(F32)
        lens = lens_ref[0, place : place + 1, :]
        count = lens // PAGE
        full += jnp.dot(count.astype(F32), want, preferred_element_type=F32)
        rest += jnp.dot((lens - count * PAGE).astype(F32), want, preferred_element_type=F32)
        pages += lax.dot_general(
            pages_ref[0, :, place, :].astype(F32), want, (((0,), (0,)), ((), ())),
            preferred_element_type=F32,
        )
    page_id = iota((POOL, 128), 0).astype(F32)
    total = jnp.zeros((POOL, 128), F32)
    last = jnp.full((1, 128), -1.0, F32)
    for j in range(CTX // PAGE):
        page = pages[j : j + 1, :]
        total += jnp.where(page_id == jnp.where(full > j, page, -1.0), 1.0, 0.0)
        last = jnp.where(full == j, page, last)

    def bias(count):
        return jnp.where(count > 0.0, jnp.log2(jnp.maximum(count, 1.0)) * BIAS, NEG)

    bias_ref[0] = bias(total)
    bias_ref[1] = bias(total + jnp.where(page_id == last, 1.0, 0.0))
    rest_ref[...] = rest
    for k in range(4):
        fetch(k).wait()
    for k in range(4):
        for e in range(8 * k, 8 * k + 8):
            packed[e] = states[slot_ref[0, e % CAP, second_peer(e // CAP)]].astype(BF)
        give(k).start()
    for k in range(4):
        give(k).wait()


def prepare(slots, owner, pos, pages, lens, ssm_pool):
    return pl.pallas_call(
        prepare_kernel,
        out_shape=(
            jax.ShapeDtypeStruct((ENT, NS, WIDE), BF),
            jax.ShapeDtypeStruct((2, POOL, 128), F32),
            jax.ShapeDtypeStruct((1, 128), F32),
            jax.ShapeDtypeStruct((ROWS,), I32),
            jax.ShapeDtypeStruct((ROWS,), I32),
        ),
        in_specs=[HB] * 6,
        out_specs=(HB, VM, VM, SM, SM),
        scratch_shapes=[
            pltpu.SMEM((1, CAP, PEERS), I32),
            pltpu.SMEM((ROWS,), I32),
            pltpu.SMEM((ROWS,), I32),
            pltpu.VMEM((1, PEERS, CAP, CTX // PAGE), I32),
            pltpu.VMEM((1, CAP, PEERS), I32),
            pltpu.VMEM((ENT, NS, EC), F32),
            pltpu.VMEM((ENT, NS, EC), BF),
            pltpu.SemaphoreType.DMA((5,)),
            pltpu.SemaphoreType.DMA((4,)),
            pltpu.SemaphoreType.DMA((4,)),
        ],
        compiler_params=ALONE,
        cost_estimate=cost(1 << 20, 6 << 20),
        name="prepare_owner",
    )(slots, owner, pos, pages, lens, ssm_pool)


PARTS = 4


def serve_kernel(
    recv_hbm, bias_hbm, rest_hbm, pool_hbm, send_ref, out_ref,
    recv_ref, bias_ref, rest_ref, pool_ref, scores, back, slab, sems,
):
    loads = [
        pltpu.make_async_copy(recv_hbm, recv_ref, sems.at[0]),
        pltpu.make_async_copy(bias_hbm, bias_ref, sems.at[1]),
        pltpu.make_async_copy(rest_hbm, rest_ref, sems.at[2]),
    ]
    for k in range(PARTS):
        part = slice(k * POOL // PARTS, (k + 1) * POOL // PARTS)
        loads.append(pltpu.make_async_copy(pool_hbm.at[part], pool_ref.at[part], sems.at[3 + k]))
    for copy in loads:
        copy.start()
    lane = iota((ENT, 256), 1)
    entry = iota((ENT, 256), 0)
    entry = CAP * first_chunk(second_peer(entry // CAP)) + entry % CAP
    pick = (lane == 8 * entry + 6).astype(F32).astype(BF)
    loads[0].wait()
    recv = recv_ref[...].reshape(256, HALF)
    query = jnp.dot(pick, recv, preferred_element_type=F32).astype(BF)
    query = jnp.concatenate([query[:, h * HD : (h + 1) * HD] for h in range(HEADS)], axis=0)
    scale = LOG2E / math.sqrt(HD)
    pages = CHUNK // PAGE
    loads[1].wait()
    loads[2].wait()
    held = iota((PAGE, 128), 0).astype(F32) < rest_ref[...]

    top = jnp.full((8, 256), NEG, F32)
    for c in range(TOK // CHUNK):
        if c % (TOK // CHUNK // PARTS) == 0:
            loads[3 + c // (TOK // CHUNK // PARTS)].wait()
        keys = pool_ref[c * pages : (c + 1) * pages, :, 0:HD].reshape(CHUNK, HD)
        raw = lax.dot_general(keys, query, (((1,), (1,)), ((), ())), preferred_element_type=F32)
        bias = jnp.concatenate(
            [
                jnp.where(held, bias_ref[1, p : p + 1, :], bias_ref[0, p : p + 1, :])
                for p in range(c * pages, (c + 1) * pages)
            ],
            axis=0,
        )
        raw = raw + jnp.concatenate([bias, bias], axis=1)
        scores[c * CHUNK : (c + 1) * CHUNK, :] = raw
        top = jnp.maximum(top, jnp.max(raw.reshape(CHUNK // 8, 8, 256), axis=0))
    top = jnp.max(top, axis=0, keepdims=True)

    mix = jnp.zeros((HD, 256), F32)
    total = jnp.zeros((8, 256), F32)
    for c in range(TOK // CHUNK):
        raw = scores[c * CHUNK : (c + 1) * CHUNK, :]
        prob = jnp.exp2((raw - top) * scale).astype(BF)
        total += jnp.sum(prob.astype(F32).reshape(CHUNK // 8, 8, 256), axis=0)
        mix += lax.dot_general(
            pool_ref[c * pages : (c + 1) * pages, :, HD:].reshape(CHUNK, HD), prob,
            (((0,), (0,)), ((), ())), preferred_element_type=F32,
        )
    total = jnp.sum(total, axis=0, keepdims=True)
    lse = top * (1.0 / math.sqrt(HD)) + jnp.log(total)
    high = lse.astype(BF).astype(F32)
    mid = (lse - high).astype(BF).astype(F32)
    low = lse - high - mid
    row = iota((HD, 256), 0)
    pieces = jnp.where(row < 32, high, jnp.where(row < 64, mid, low)).T
    mix = (mix * (1.0 / total)).T
    for h in range(HEADS):
        back[pl.ds(h, ENT, 16), :] = mix[h * ENT : (h + 1) * ENT, :]
        back[pl.ds(8 + h, ENT, 16), :] = pieces[h * ENT : (h + 1) * ENT, :]
    slab[...] = back[...].astype(BF).reshape(ENT, 16, HD)
    copy = pltpu.make_async_copy(slab, out_ref.at[:, :, EC:WIDE], sems.at[0])
    copy.start()
    copy.wait()


def serve(recv, bias, rest, kv_pool, send):
    return pl.pallas_call(
        serve_kernel,
        out_shape=jax.ShapeDtypeStruct((ENT, NS, WIDE), BF),
        in_specs=[HB] * 4 + [AN],
        out_specs=AN,
        input_output_aliases={4: 0},
        scratch_shapes=[
            pltpu.VMEM((PEERS, 16, HALF), BF),
            pltpu.VMEM((2, POOL, 128), F32),
            pltpu.VMEM((1, 128), F32),
            pltpu.VMEM((POOL, PAGE, 2 * HD), BF),
            pltpu.VMEM((TOK, 256), F32),
            pltpu.VMEM((ENT * 16, HD), F32),
            pltpu.VMEM((ENT, 16, HD), BF),
            pltpu.SemaphoreType.DMA((3 + PARTS,)),
        ],
        compiler_params=ALONE,
        cost_estimate=cost(4 * TOK * 256 * HD, 6 << 20),
        name="serve_pool",
    )(recv, bias, rest, kv_pool, send)


BLK = 8


def resident_kernel(
    after_ref, len_ref, query_ref, new_ref, cache_ref, mix_ref, score_ref, heads
):
    step = pl.program_id(0)

    @pl.when(step == 0)
    def _():
        for h in range(HEADS):
            heads[pl.ds(h, ROWS, 8), :] = query_ref[:, h * HD : (h + 1) * HD].astype(F32)

    scale = LOG2E / math.sqrt(HD)
    rows = BLK * 8
    wide = heads[pl.ds(pl.multiple_of(step * rows, rows), rows), :]
    query = wide.astype(BF)
    raw = []
    lens = []
    for b in range(BLK):
        raw.append(
            lax.dot_general(
                query[8 * b : 8 * b + 8], cache_ref[b, :, 0:HD], (((1,), (1,)), ((), ())),
                preferred_element_type=F32,
            )
        )
        lens.append(jnp.full((8, CTX), len_ref[step * BLK + b], I32))
    raw = jnp.concatenate(raw, axis=0)
    live = iota((rows, CTX), 1) < jnp.concatenate(lens, axis=0)
    raw = jnp.where(live, raw * scale, NEG)
    top = jnp.max(raw, axis=1, keepdims=True)
    prob = jnp.exp2(raw - top).astype(BF)
    total = jnp.sum(prob.astype(F32), axis=1, keepdims=True)
    mix = jnp.concatenate(
        [
            jnp.dot(prob[8 * b : 8 * b + 8], cache_ref[b, :, HD:], preferred_element_type=F32)
            for b in range(BLK)
        ],
        axis=0,
    )
    new = new_ref[...].astype(F32)
    key = jnp.concatenate(
        [jnp.broadcast_to(new[b : b + 1, 0:HD], (8, HD)) for b in range(BLK)], axis=0
    )
    value = jnp.concatenate(
        [jnp.broadcast_to(new[b : b + 1, HD:], (8, HD)) for b in range(BLK)], axis=0
    )
    score = jnp.sum(wide * key, axis=1, keepdims=True) * scale
    peak = jnp.maximum(top, score)
    old = jnp.exp2(top - peak)
    add = jnp.exp2(score - peak)
    mix_ref[...] = (mix * old + add * value) / (total * old + add)
    score_ref[...] = jnp.broadcast_to(score * LN2, (rows, HD))


def resident(after, lens, query, new_kv, kv_cache):
    tile = pl.BlockSpec((BLK * 8, HD), lambda i: (i, 0))
    shape = jax.ShapeDtypeStruct((ROWS * 8, HD), F32)
    return pl.pallas_call(
        resident_kernel,
        grid=(ROWS // BLK,),
        out_shape=(shape, shape),
        in_specs=[
            AN,
            SM,
            pl.BlockSpec((ROWS, HEADS * HD), lambda i: (0, 0)),
            pl.BlockSpec((BLK, 2 * HD), lambda i: (i, 0)),
            pl.BlockSpec((BLK, CTX, 2 * HD), lambda i: (i, 0, 0)),
        ],
        out_specs=(tile, tile),
        scratch_shapes=[pltpu.VMEM((ROWS * 8, HD), F32)],
        compiler_params=params(58),
        cost_estimate=cost(4 * ROWS * 8 * CTX * HD, 9 << 20),
        name="resident_attention",
    )(after, lens, query, new_kv, kv_cache)


def mix_kernel(
    after_ref, source_ref, recv_ref, conv_ref, x_ref, weight_ref, bias_ref, proj_ref,
    mixed_ref, window_ref, part_ref, send_ref,
):
    sub = iota((ROWS, 256), 0)
    lane = iota((ROWS, 256), 1)
    source = jnp.full((ROWS, 256), -1, I32)
    for r in range(ROWS):
        source = jnp.where(sub == r, source_ref[r], source)
    base = jnp.where(source >= 0, source * 8, -8)
    pick = jnp.concatenate([(lane == base + k).astype(F32) for k in range(6)], axis=0).astype(BF)
    recv = recv_ref[...].reshape(256, HALF)
    prev = jnp.dot(pick, recv, preferred_element_type=F32)
    came = source[:, 0:1] >= 0
    x = x_ref[...]
    total = x.astype(F32) * weight_ref[3:4, :].astype(F32)
    window_ref[2] = x
    for j in range(3):
        here = jnp.concatenate(
            [prev[64 * j : 64 * j + 32], prev[64 * j + 32 : 64 * j + 64]], axis=1
        )
        tap = jnp.where(came, here, conv_ref[j].astype(F32))
        if j > 0:
            window_ref[j - 1] = tap.astype(BF)
        total += tap * weight_ref[j : j + 1, :].astype(F32)
    total += bias_ref[...]
    mixed = (total / (1.0 + jnp.exp(-total))).astype(BF)
    mixed_ref[...] = mixed
    part = lax.dot_general(
        mixed, proj_ref[...], (((1,), (1,)), ((), ())), preferred_element_type=F32
    )
    part_ref[...] = part
    send_ref[...] = part.astype(BF)


def mix(after, source, recv, conv_state, x_in, weight, bias, proj_t):
    wide = proj_t.shape[0]
    return pl.pallas_call(
        mix_kernel,
        out_shape=(
            jax.ShapeDtypeStruct((ROWS, EC), BF),
            jax.ShapeDtypeStruct((3, ROWS, EC), BF),
            jax.ShapeDtypeStruct((ROWS, wide), F32),
            jax.ShapeDtypeStruct((ROWS, wide), BF),
        ),
        in_specs=[AN, SM] + [VM] * 6,
        out_specs=(VM, VM, VM, VM),
        compiler_params=ALONE,
        cost_estimate=cost(2 * ROWS * EC * wide, 4 << 20),
        name="mix_input",
    )(after, source, recv, conv_state, x_in, weight, bias, proj_t)


GROUP = 8


def advance(prev, dt, decay, drive, inject):
    return jnp.exp2(dt * decay) * prev + drive * inject


def step_kernel(*refs):
    source_ref, part_ref = refs[0:2]
    others = refs[2:9]
    (
        gain_ref, b_gain_ref, c_gain_ref, proj_ref, bias_ref, mixed_ref, skip_ref, z_ref, decay_ref, state_ref,
        dt_ref, drive_ref, inject_ref, read_ref, gate_ref, base_ref, new_ref,
        local, made, flat, in_sems, out_sems,
    ) = refs[9:]

    def fetch(r):
        return pltpu.make_async_copy(state_ref.at[r], local.at[r], in_sems.at[r])

    def store(r):
        return pltpu.make_async_copy(made.at[r], new_ref.at[r], out_sems.at[r])

    for r in range(ROWS):

        @pl.when(source_ref[r] < 0)
        def _():
            fetch(r).start()

    proj = part_ref[...]
    for other in others:
        proj += other[...].astype(F32)
    low = proj[:, 0:RANK]
    mean = jnp.sum(low * low, axis=1, keepdims=True) * (1.0 / RANK)
    normed = (low * lax.rsqrt(mean + 1e-6) * gain_ref[...]).astype(BF)
    dt = jnp.dot(normed, proj_ref[...], preferred_element_type=F32) + bias_ref[...]
    dt = jnp.maximum(dt, 0.0) + jnp.log1p(jnp.exp(-jnp.abs(dt)))
    mixed = mixed_ref[...].astype(F32)
    drive = dt * mixed
    dt = dt * (-LOG2E)
    for r in range(ROWS):
        dt_ref[r] = dt[r : r + 1, :]
        drive_ref[r] = drive[r : r + 1, :]
    z = z_ref[...].astype(F32)
    gate = z / (1.0 + jnp.exp(-z))
    gate_ref[...] = gate
    base_ref[...] = skip_ref[...] * mixed * gate
    tail = proj[:, RANK : RANK + 2 * NS]
    square = tail * tail
    front = iota((ROWS, 2 * NS), 1) < NS
    mean_b = jnp.sum(jnp.where(front, square, 0.0), axis=1, keepdims=True) * (1.0 / NS)
    mean_c = jnp.sum(jnp.where(front, 0.0, square), axis=1, keepdims=True) * (1.0 / NS)
    scale = lax.rsqrt(jnp.where(front, mean_b, mean_c) + 1e-6)
    tail_gain = jnp.concatenate([b_gain_ref[...], c_gain_ref[...]], axis=1)
    tail = (tail * scale * tail_gain).astype(BF)
    lane = iota((2 * NS, 128), 1)
    spread = (iota((2 * NS, 128), 0) == NS + lane % NS).astype(F32).astype(BF)
    read = jnp.dot(tail, spread, preferred_element_type=F32)
    own = iota((ROWS, 128), 1) // NS == iota((ROWS, 128), 0) % GROUP
    read_ref[...] = jnp.where(own, read, 0.0)
    many = (iota((ROWS * NS, ROWS), 0) // NS == iota((ROWS * NS, ROWS), 1)).astype(F32).astype(BF)
    each = jnp.dot(many, tail, preferred_element_type=F32)
    mine = iota((ROWS * NS, 2 * NS), 0) % NS == iota((ROWS * NS, 2 * NS), 1)
    each = jnp.where(mine, each, 0.0).astype(BF)
    inject = jnp.dot(each, jnp.ones((2 * NS, 128), BF), preferred_element_type=F32)
    inject_ref[...] = inject.reshape(ROWS, NS, 128)

    def body(i, carry):
        for b in range(GROUP):
            r = i * GROUP + b

            @pl.when(source_ref[r] < 0)
            def _():
                fetch(r).wait()
                inject = jnp.concatenate([inject_ref[r]] * 4, axis=1)
                for c in range(EC // 512):
                    cols = slice(c * 512, (c + 1) * 512)
                    new = advance(
                        local[r, :, cols], dt_ref[r, :, cols], decay_ref[:, cols],
                        drive_ref[r, :, cols], inject,
                    )
                    made[r, :, cols] = new
                    flat[b * NS : (b + 1) * NS, cols] = new.astype(BF)
                store(r).start()

            @pl.when(source_ref[r] >= 0)
            def _():
                flat[b * NS : (b + 1) * NS, :] = jnp.zeros((NS, EC), BF)

        rows = pl.ds(pl.multiple_of(i * GROUP, GROUP), GROUP)
        sums = jnp.dot(read_ref[rows, :].astype(BF), flat[...], preferred_element_type=F32)
        base_ref[rows, :] += sums * gate_ref[rows, :]
        return carry

    lax.fori_loop(0, ROWS // GROUP, body, 0)
    for r in range(ROWS):

        @pl.when(source_ref[r] < 0)
        def _():
            store(r).wait()


def step_size(source, part, others, *operands):
    return pl.pallas_call(
        step_kernel,
        out_shape=(
            jax.ShapeDtypeStruct((ROWS, 1, EC), F32),
            jax.ShapeDtypeStruct((ROWS, 1, EC), F32),
            jax.ShapeDtypeStruct((ROWS, NS, 128), F32),
            jax.ShapeDtypeStruct((ROWS, 128), F32),
            jax.ShapeDtypeStruct((ROWS, EC), F32),
            jax.ShapeDtypeStruct((ROWS, EC), F32),
            jax.ShapeDtypeStruct((ROWS, NS, EC), F32),
        ),
        in_specs=[SM] + [VM] * 17 + [HB],
        out_specs=(VM,) * 6 + (HB,),
        scratch_shapes=[
            pltpu.VMEM((ROWS, NS, EC), F32),
            pltpu.VMEM((ROWS, NS, EC), F32),
            pltpu.VMEM((GROUP * NS, EC), BF),
            pltpu.SemaphoreType.DMA((ROWS,)),
            pltpu.SemaphoreType.DMA((ROWS,)),
        ],
        compiler_params=params(56),
        cost_estimate=cost(2 * ROWS * EC * RANK, 12 << 20),
        name="step_and_resident",
    )(source, part, *others, *operands)


def tail_kernel(
    source_ref, came, dt_ref, drive_ref, inject_ref, read_ref, decay_ref,
    gate_ref, base_ref, mix_ref, score_ref, new_kv_ref, kept_ref,
    new_ref, out_hbm, attn_hbm,
    out_ref, attn_ref, made, flat, sums, other, pieces, sems, out_sems,
):
    def store(r):
        return pltpu.make_async_copy(made.at[r], new_ref.at[r], out_sems.at[r])

    def store_all(i):
        rows = pl.ds(pl.multiple_of(i * GROUP, GROUP), GROUP)
        return pltpu.make_async_copy(made.at[rows], new_ref.at[rows], out_sems.at[i * GROUP])

    def leave(i, act):
        count = jnp.int32(0)
        for b in range(GROUP):
            count += jnp.where(source_ref[i * GROUP + b] >= 0, 1, 0)

        @pl.when(count == GROUP)
        def _():
            act(store_all(i))

        @pl.when(count < GROUP)
        def _():
            for b in range(GROUP):
                r = i * GROUP + b

                @pl.when(source_ref[r] >= 0)
                def _():
                    act(store(r))

    lane = iota((8, HD), 1)
    huge = jnp.where(lane < 32, -NEG, 0.0)

    def body(i, carry):
        for b in range(GROUP):
            r = i * GROUP + b
            source = source_ref[r]
            here = pl.ds(pl.multiple_of(8 * r, 8), 8)

            @pl.when(source >= 0)
            def _():
                tile = came[source, :, EC:WIDE].astype(F32)
                other[here, :] = tile[0:8, :]
                pieces[here, :] = tile[8:16, :]
                inject = jnp.concatenate([inject_ref[r]] * 4, axis=1)
                for c in range(EC // 512):
                    cols = slice(c * 512, (c + 1) * 512)
                    new = advance(
                        came[source, :, cols].astype(F32), dt_ref[r, :, cols],
                        decay_ref[:, cols], drive_ref[r, :, cols], inject,
                    )
                    made[r, :, cols] = new
                    flat[b * NS : (b + 1) * NS, cols] = new.astype(BF)

            @pl.when(source < 0)
            def _():
                other[here, :] = mix_ref[here, :]
                pieces[here, :] = huge
                flat[b * NS : (b + 1) * NS, :] = jnp.zeros((NS, EC), BF)

        leave(i, lambda copy: copy.start())
        rows = pl.ds(pl.multiple_of(i * GROUP, GROUP), GROUP)
        sums[rows, :] = jnp.dot(
            read_ref[rows, :].astype(BF), flat[...], preferred_element_type=F32
        )
        return carry

    lax.fori_loop(0, ROWS // GROUP, body, 0)
    out_ref[...] = (sums[...] * gate_ref[...] + base_ref[...]).astype(BF)
    give_out = pltpu.make_async_copy(out_ref, out_hbm, sems.at[0])
    give_out.start()
    lse = pieces[:, 0:1] + pieces[:, 32:33] + pieces[:, 64:65]
    score = score_ref[...]
    peak = jnp.maximum(lse, score)
    old = jnp.exp(lse - peak)
    new = jnp.exp(score - peak)
    value = new_kv_ref[:, HD:].astype(F32)
    value = jnp.concatenate(
        [jnp.broadcast_to(value[r : r + 1, :], (8, HD)) for r in range(ROWS)], axis=0
    )
    pieces[...] = (other[...] * old + new * value) / (old + new)
    for h in range(HEADS):
        attn_ref[:, h * HD : (h + 1) * HD] = pieces[pl.ds(h, ROWS, 8), :].astype(BF)
    give_attn = pltpu.make_async_copy(attn_ref, attn_hbm, sems.at[1])
    give_attn.start()
    give_out.wait()
    give_attn.wait()
    for i in range(ROWS // GROUP):
        leave(i, lambda copy: copy.wait())


def tail(*operands):
    return pl.pallas_call(
        tail_kernel,
        out_shape=(
            jax.ShapeDtypeStruct((ROWS, NS, EC), F32),
            jax.ShapeDtypeStruct((ROWS, EC), BF),
            jax.ShapeDtypeStruct((ROWS, HEADS * HD), BF),
        ),
        in_specs=[SM] + [VM] * 11 + [AN],
        out_specs=(AN, HB, HB),
        input_output_aliases={12: 0},
        scratch_shapes=[
            pltpu.VMEM((ROWS, EC), BF),
            pltpu.VMEM((ROWS, HEADS * HD), BF),
            pltpu.VMEM((ROWS, NS, EC), F32),
            pltpu.VMEM((GROUP * NS, EC), BF),
            pltpu.VMEM((ROWS, EC), F32),
            pltpu.VMEM((ROWS * 8, HD), F32),
            pltpu.VMEM((ROWS * 8, HD), F32),
            pltpu.SemaphoreType.DMA((10,)),
            pltpu.SemaphoreType.DMA((ROWS,)),
        ],
        compiler_params=ALONE,
        cost_estimate=cost(16 << 20, 8 << 20),
        name="update_and_join",
    )(*operands)


def swap(values, order):
    return lax.all_to_all(
        values, "rep", split_axis=0, concat_axis=0, tiled=True, axis_index_groups=[order]
    )


def shards(
    x_in, z_gate, conv_state, conv_pool, ssm_state, ssm_pool, conv_weight, conv_bias, x_proj,
    dt_gain, b_gain, c_gain, dt_proj, dt_bias, decay_rate, skip, query, new_kv, kv_cache, kv_pool,
    ctx_len, row_owner, row_pos, swap_slot, swap_lens, swap_pages,
):
    slots = swap_slot.transpose(0, 2, 1)
    firsts = [first_peer(p) for p in range(PEERS)]
    seconds = [second_peer(p) for p in range(PEERS)]
    first = swap(pack(slots, row_owner, row_pos, conv_pool.transpose(1, 0, 2), query), firsts)
    states, bias, rest, source, state_source = prepare(
        slots, row_owner, row_pos, swap_pages, swap_lens.transpose(0, 2, 1), ssm_pool
    )
    states = serve(first, bias, rest, kv_pool, states)
    second = swap(states.reshape(PEERS, CAP * NS, WIDE), seconds).reshape(ENT, NS, WIDE)

    mixed, window, part, send = mix(
        states, source, first, conv_state.transpose(1, 0, 2), x_in, conv_weight,
        conv_bias.reshape(1, EC), x_proj.T,
    )
    tp = lax.axis_size("tp")
    others = [
        lax.ppermute(send, "tp", [(i, (i + s) % tp) for i in range(tp)]) for s in range(1, tp)
    ]
    mix_here, score = resident(states, ctx_len, query, new_kv, kv_cache)
    dt, drive, inject, read, gate, base, kept = step_size(
        state_source, part, others, dt_gain.reshape(1, RANK),
        b_gain.reshape(1, NS), c_gain.reshape(1, NS), dt_proj, dt_bias.reshape(1, EC), mixed,
        skip.reshape(1, EC), z_gate, decay_rate, ssm_state,
    )
    new_ssm, mamba_out, attn_out = tail(
        state_source, second, dt, drive, inject, read, decay_rate, gate, base, mix_here, score, new_kv, kept
    )
    return (mamba_out, attn_out, new_ssm, window.transpose(1, 0, 2))


def solution(mesh):
    in_specs = (
        P("rep", "tp"), P("rep", "tp"), P("rep", None, "tp"), P("rep", None, "tp"),
        P("rep", None, "tp"), P("rep", None, "tp"), P(None, "tp"), P("tp"), P("tp", None),
        P(), P(), P(), P(None, "tp"), P("tp"), P(None, "tp"), P("tp"), P("rep", "tp"),
        P("rep", "tp"), P("rep", None, "tp"), P("rep", None, "tp"), P("rep"), P("rep"), P("rep"),
        P("rep", None, None), P("rep", None, None), P("rep", None, None, None),
    )
    out_specs = (P("rep", "tp"), P("rep", "tp"), P("rep", None, "tp"), P("rep", None, "tp"))
    return jax.shard_map(shards, mesh=mesh, in_specs=in_specs, out_specs=out_specs, check_vma=False)
```

```python
import functools
import math

import jax
import jax.numpy as jnp
from jax import lax
from jax.experimental import pallas as pl
from jax.experimental.pallas import tpu as pltpu
from jax.sharding import PartitionSpec as P

BF = jnp.bfloat16
F32 = jnp.float32
I32 = jnp.int32
PEERS = 16
CAP = 2
SIDE = 4
ENT = PEERS * CAP
ROWS = 32
EC = 2048
HALF = EC // 2
NS = 16
RANK = 512
HEADS = 8
HD = 128
CTX = 512
PAGE = 16
POOL = 256
TOK = POOL * PAGE
CHUNK = 256
LOG2E = 1.4426950408889634
LN2 = 0.6931471805599453
NEG = -1e30

VM = pl.BlockSpec(memory_space=pltpu.VMEM)
SM = pl.BlockSpec(memory_space=pltpu.SMEM)
AN = pl.BlockSpec(memory_space=pl.ANY)
HB = pl.BlockSpec(memory_space=pltpu.HBM)
WIDE = EC + HD
BIAS = math.sqrt(HD) / LOG2E


def iota(shape, dim):
    return lax.broadcasted_iota(I32, shape, dim)


def first_peer(chunk):
    return (chunk + PEERS - SIDE) % PEERS


def first_chunk(peer):
    return (peer + SIDE) % PEERS


def second_peer(chunk):
    return PEERS - 1 - SIDE * (chunk % SIDE) - chunk // SIDE


second_chunk = second_peer


def params(mib):
    return pltpu.CompilerParams(vmem_limit_bytes=mib * 1024 * 1024)


ALONE = pltpu.CompilerParams(vmem_limit_bytes=65716224)


def cost(flops, byts):
    return pl.CostEstimate(flops=flops, bytes_accessed=byts, transcendentals=0)


def pack_kernel(
    slot_hbm, owner_hbm, pos_hbm, conv_ref, query_ref, out_ref,
    stack, made, inverse, slot_ref, owner_ref, pos_ref, sems,
):
    copies = [
        pltpu.make_async_copy(slot_hbm, slot_ref, sems.at[0]),
        pltpu.make_async_copy(owner_hbm, owner_ref, sems.at[1]),
        pltpu.make_async_copy(pos_hbm, pos_ref, sems.at[2]),
        pltpu.make_async_copy(query_ref, stack.at[192:224], sems.at[3]),
    ]
    for k in range(6):
        j, h = k // 2, k % 2
        copies.append(
            pltpu.make_async_copy(
                conv_ref.at[j, :, h * HALF : (h + 1) * HALF],
                stack.at[32 * k : 32 * k + 32],
                sems.at[4 + k],
            )
        )
    for copy in copies:
        copy.start()
    stack[224:256, :] = jnp.zeros((32, HALF), BF)
    for e in range(ENT):
        inverse[e] = -1
    for copy in copies[:3]:
        copy.wait()
    for r in range(ROWS):
        owner = owner_ref[r]

        @pl.when(owner >= 0)
        def _():
            inverse[first_chunk(owner) * CAP + pos_ref[r]] = 192 + r

    lane = iota((8, 256), 1)
    part = iota((8, 256), 0)
    tiles = []
    for e in range(ENT):
        slot = slot_ref[0, e % CAP, first_peer(e // CAP)]
        want = jnp.where(part < 6, 32 * part + slot, jnp.where(part == 6, inverse[e], -1))
        tiles.append((lane == want).astype(F32))
    pick = jnp.concatenate(tiles, axis=0).astype(BF)
    for copy in copies[3:]:
        copy.wait()
    gone = []
    for k in range(2):
        packed = jnp.dot(pick[128 * k : 128 * k + 128], stack[...], preferred_element_type=F32)
        made[8 * k : 8 * k + 8] = packed.astype(BF).reshape(8, 16, HALF)
        part = slice(8 * k, 8 * k + 8)
        gone.append(pltpu.make_async_copy(made.at[part], out_ref.at[part], sems.at[k]))
        gone[k].start()
    for copy in gone:
        copy.wait()


def pack(slots, owner, pos, conv_pool, query):
    return pl.pallas_call(
        pack_kernel,
        out_shape=jax.ShapeDtypeStruct((PEERS, 16, HALF), BF),
        in_specs=[HB] * 5,
        out_specs=HB,
        scratch_shapes=[
            pltpu.VMEM((256, HALF), BF),
            pltpu.VMEM((PEERS, 16, HALF), BF),
            pltpu.SMEM((ENT,), I32),
            pltpu.SMEM((1, CAP, PEERS), I32),
            pltpu.SMEM((ROWS,), I32),
            pltpu.SMEM((ROWS,), I32),
            pltpu.SemaphoreType.DMA((10,)),
        ],
        compiler_params=ALONE,
        cost_estimate=cost(2 * 256 * 256 * HALF, 1 << 20),
        name="pack_first",
    )(slots, owner, pos, conv_pool, query)


def prepare_kernel(
    slot_hbm, owner_hbm, pos_hbm, pages_hbm, lens_hbm, ssm_ref,
    states_ref, bias_ref, rest_ref, source_ref, state_source_ref,
    slot_ref, owner_ref, pos_ref, pages_ref, lens_ref, states, packed, sems, in_sems, out_sems,
):
    first = [
        pltpu.make_async_copy(slot_hbm, slot_ref, sems.at[0]),
        pltpu.make_async_copy(owner_hbm, owner_ref, sems.at[3]),
        pltpu.make_async_copy(pos_hbm, pos_ref, sems.at[4]),
    ]
    for copy in first:
        copy.start()
    lists = [
        pltpu.make_async_copy(pages_hbm, pages_ref, sems.at[1]),
        pltpu.make_async_copy(lens_hbm, lens_ref, sems.at[2]),
    ]
    for copy in lists:
        copy.start()
    for copy in first:
        copy.wait()

    def fetch(k):
        return pltpu.make_async_copy(
            ssm_ref.at[8 * k : 8 * k + 8], states.at[8 * k : 8 * k + 8], in_sems.at[k]
        )

    def give(k):
        return pltpu.make_async_copy(
            packed.at[8 * k : 8 * k + 8], states_ref.at[8 * k : 8 * k + 8, :, 0:EC], out_sems.at[k]
        )

    for k in range(4):
        fetch(k).start()
    for r in range(ROWS):
        resumed = owner_ref[r] >= 0
        owner = jnp.maximum(owner_ref[r], 0)
        pos = pos_ref[r]
        source_ref[r] = jnp.where(resumed, first_chunk(owner) * CAP + pos, -1)
        state_source_ref[r] = jnp.where(resumed, second_chunk(owner) * CAP + pos, -1)
    for copy in lists:
        copy.wait()

    full = jnp.zeros((1, 128), F32)
    rest = jnp.zeros((1, 128), F32)
    pages = jnp.zeros((CTX // PAGE, 128), F32)
    for place in range(CAP):
        want = iota((PEERS, 128), 1) % ENT == second_chunk(iota((PEERS, 128), 0)) * CAP + place
        want = want.astype(F32)
        lens = lens_ref[0, place : place + 1, :]
        count = lens // PAGE
        full += jnp.dot(count.astype(F32), want, preferred_element_type=F32)
        rest += jnp.dot((lens - count * PAGE).astype(F32), want, preferred_element_type=F32)
        pages += lax.dot_general(
            pages_ref[0, :, place, :].astype(F32), want, (((0,), (0,)), ((), ())),
            preferred_element_type=F32,
        )
    page_id = iota((POOL, 128), 0).astype(F32)
    total = jnp.zeros((POOL, 128), F32)
    last = jnp.full((1, 128), -1.0, F32)
    for j in range(CTX // PAGE):
        page = pages[j : j + 1, :]
        total += jnp.where(page_id == jnp.where(full > j, page, -1.0), 1.0, 0.0)
        last = jnp.where(full == j, page, last)

    def bias(count):
        return jnp.where(count > 0.0, jnp.log2(jnp.maximum(count, 1.0)) * BIAS, NEG)

    bias_ref[0] = bias(total)
    bias_ref[1] = bias(total + jnp.where(page_id == last, 1.0, 0.0))
    rest_ref[...] = rest
    for k in range(4):
        fetch(k).wait()
    for k in range(4):
        for e in range(8 * k, 8 * k + 8):
            packed[e] = states[slot_ref[0, e % CAP, second_peer(e // CAP)]].astype(BF)
        give(k).start()
    for k in range(4):
        give(k).wait()


def prepare(slots, owner, pos, pages, lens, ssm_pool):
    return pl.pallas_call(
        prepare_kernel,
        out_shape=(
            jax.ShapeDtypeStruct((ENT, NS, WIDE), BF),
            jax.ShapeDtypeStruct((2, POOL, 128), F32),
            jax.ShapeDtypeStruct((1, 128), F32),
            jax.ShapeDtypeStruct((ROWS,), I32),
            jax.ShapeDtypeStruct((ROWS,), I32),
        ),
        in_specs=[HB] * 6,
        out_specs=(HB, VM, VM, SM, SM),
        scratch_shapes=[
            pltpu.SMEM((1, CAP, PEERS), I32),
            pltpu.SMEM((ROWS,), I32),
            pltpu.SMEM((ROWS,), I32),
            pltpu.VMEM((1, PEERS, CAP, CTX // PAGE), I32),
            pltpu.VMEM((1, CAP, PEERS), I32),
            pltpu.VMEM((ENT, NS, EC), F32),
            pltpu.VMEM((ENT, NS, EC), BF),
            pltpu.SemaphoreType.DMA((5,)),
            pltpu.SemaphoreType.DMA((4,)),
            pltpu.SemaphoreType.DMA((4,)),
        ],
        compiler_params=ALONE,
        cost_estimate=cost(1 << 20, 6 << 20),
        name="prepare_owner",
    )(slots, owner, pos, pages, lens, ssm_pool)


PARTS = 2


def serve_kernel(
    recv_hbm, bias_hbm, rest_hbm, pool_hbm, send_ref, out_ref,
    recv_ref, bias_ref, rest_ref, pool_ref, scores, back, slab, sems,
):
    loads = [
        pltpu.make_async_copy(recv_hbm, recv_ref, sems.at[0]),
        pltpu.make_async_copy(bias_hbm, bias_ref, sems.at[1]),
        pltpu.make_async_copy(rest_hbm, rest_ref, sems.at[2]),
    ]
    for k in range(PARTS):
        part = slice(k * POOL // PARTS, (k + 1) * POOL // PARTS)
        loads.append(pltpu.make_async_copy(pool_hbm.at[part], pool_ref.at[part], sems.at[3 + k]))
    for copy in loads:
        copy.start()
    lane = iota((ENT, 256), 1)
    entry = iota((ENT, 256), 0)
    entry = CAP * first_chunk(second_peer(entry // CAP)) + entry % CAP
    pick = (lane == 8 * entry + 6).astype(F32).astype(BF)
    loads[0].wait()
    recv = recv_ref[...].reshape(256, HALF)
    query = jnp.dot(pick, recv, preferred_element_type=F32).astype(BF)
    query = jnp.concatenate([query[:, h * HD : (h + 1) * HD] for h in range(HEADS)], axis=0)
    scale = LOG2E / math.sqrt(HD)
    pages = CHUNK // PAGE
    loads[1].wait()
    loads[2].wait()
    held = iota((PAGE, 128), 0).astype(F32) < rest_ref[...]

    top = jnp.full((8, 256), NEG, F32)
    for c in range(TOK // CHUNK):
        if c % (TOK // CHUNK // PARTS) == 0:
            loads[3 + c // (TOK // CHUNK // PARTS)].wait()
        keys = pool_ref[c * pages : (c + 1) * pages, :, 0:HD].reshape(CHUNK, HD)
        raw = lax.dot_general(keys, query, (((1,), (1,)), ((), ())), preferred_element_type=F32)
        bias = jnp.concatenate(
            [
                jnp.where(held, bias_ref[1, p : p + 1, :], bias_ref[0, p : p + 1, :])
                for p in range(c * pages, (c + 1) * pages)
            ],
            axis=0,
        )
        raw = raw + jnp.concatenate([bias, bias], axis=1)
        scores[c * CHUNK : (c + 1) * CHUNK, :] = raw
        top = jnp.maximum(top, jnp.max(raw.reshape(CHUNK // 8, 8, 256), axis=0))
    top = jnp.max(top, axis=0, keepdims=True)

    mix = jnp.zeros((HD, 256), F32)
    total = jnp.zeros((8, 256), F32)
    for c in range(TOK // CHUNK):
        raw = scores[c * CHUNK : (c + 1) * CHUNK, :]
        prob = jnp.exp2((raw - top) * scale).astype(BF)
        total += jnp.sum(prob.astype(F32).reshape(CHUNK // 8, 8, 256), axis=0)
        mix += lax.dot_general(
            pool_ref[c * pages : (c + 1) * pages, :, HD:].reshape(CHUNK, HD), prob,
            (((0,), (0,)), ((), ())), preferred_element_type=F32,
        )
    total = jnp.sum(total, axis=0, keepdims=True)
    lse = top * (1.0 / math.sqrt(HD)) + jnp.log(total)
    high = lse.astype(BF).astype(F32)
    mid = (lse - high).astype(BF).astype(F32)
    low = lse - high - mid
    row = iota((HD, 256), 0)
    pieces = jnp.where(row < 32, high, jnp.where(row < 64, mid, low)).T
    mix = (mix * (1.0 / total)).T
    for h in range(HEADS):
        back[pl.ds(h, ENT, 16), :] = mix[h * ENT : (h + 1) * ENT, :]
        back[pl.ds(8 + h, ENT, 16), :] = pieces[h * ENT : (h + 1) * ENT, :]
    slab[...] = back[...].astype(BF).reshape(ENT, 16, HD)
    copy = pltpu.make_async_copy(slab, out_ref.at[:, :, EC:WIDE], sems.at[0])
    copy.start()
    copy.wait()


def serve(recv, bias, rest, kv_pool, send):
    return pl.pallas_call(
        serve_kernel,
        out_shape=jax.ShapeDtypeStruct((ENT, NS, WIDE), BF),
        in_specs=[HB] * 4 + [AN],
        out_specs=AN,
        input_output_aliases={4: 0},
        scratch_shapes=[
            pltpu.VMEM((PEERS, 16, HALF), BF),
            pltpu.VMEM((2, POOL, 128), F32),
            pltpu.VMEM((1, 128), F32),
            pltpu.VMEM((POOL, PAGE, 2 * HD), BF),
            pltpu.VMEM((TOK, 256), F32),
            pltpu.VMEM((ENT * 16, HD), F32),
            pltpu.VMEM((ENT, 16, HD), BF),
            pltpu.SemaphoreType.DMA((3 + PARTS,)),
        ],
        compiler_params=ALONE,
        cost_estimate=cost(4 * TOK * 256 * HD, 6 << 20),
        name="serve_pool",
    )(recv, bias, rest, kv_pool, send)


BLK = 8


def resident_kernel(
    after_ref, len_ref, query_ref, new_ref, cache_ref, mix_ref, score_ref, heads
):
    step = pl.program_id(0)

    @pl.when(step == 0)
    def _():
        for h in range(HEADS):
            heads[pl.ds(h, ROWS, 8), :] = query_ref[:, h * HD : (h + 1) * HD].astype(F32)

    scale = LOG2E / math.sqrt(HD)
    rows = BLK * 8
    wide = heads[pl.ds(pl.multiple_of(step * rows, rows), rows), :]
    query = wide.astype(BF)
    raw = []
    lens = []
    for b in range(BLK):
        raw.append(
            lax.dot_general(
                query[8 * b : 8 * b + 8], cache_ref[b, :, 0:HD], (((1,), (1,)), ((), ())),
                preferred_element_type=F32,
            )
        )
        lens.append(jnp.full((8, CTX), len_ref[step * BLK + b], I32))
    raw = jnp.concatenate(raw, axis=0)
    live = iota((rows, CTX), 1) < jnp.concatenate(lens, axis=0)
    raw = jnp.where(live, raw * scale, NEG)
    top = jnp.max(raw, axis=1, keepdims=True)
    prob = jnp.exp2(raw - top).astype(BF)
    total = jnp.sum(prob.astype(F32), axis=1, keepdims=True)
    mix = jnp.concatenate(
        [
            jnp.dot(prob[8 * b : 8 * b + 8], cache_ref[b, :, HD:], preferred_element_type=F32)
            for b in range(BLK)
        ],
        axis=0,
    )
    new = new_ref[...].astype(F32)
    key = jnp.concatenate(
        [jnp.broadcast_to(new[b : b + 1, 0:HD], (8, HD)) for b in range(BLK)], axis=0
    )
    value = jnp.concatenate(
        [jnp.broadcast_to(new[b : b + 1, HD:], (8, HD)) for b in range(BLK)], axis=0
    )
    score = jnp.sum(wide * key, axis=1, keepdims=True) * scale
    peak = jnp.maximum(top, score)
    old = jnp.exp2(top - peak)
    add = jnp.exp2(score - peak)
    mix_ref[...] = (mix * old + add * value) / (total * old + add)
    score_ref[...] = jnp.broadcast_to(score * LN2, (rows, HD))


def resident(after, lens, query, new_kv, kv_cache):
    tile = pl.BlockSpec((BLK * 8, HD), lambda i: (i, 0))
    shape = jax.ShapeDtypeStruct((ROWS * 8, HD), F32)
    return pl.pallas_call(
        resident_kernel,
        grid=(ROWS // BLK,),
        out_shape=(shape, shape),
        in_specs=[
            AN,
            SM,
            pl.BlockSpec((ROWS, HEADS * HD), lambda i: (0, 0)),
            pl.BlockSpec((BLK, 2 * HD), lambda i: (i, 0)),
            pl.BlockSpec((BLK, CTX, 2 * HD), lambda i: (i, 0, 0)),
        ],
        out_specs=(tile, tile),
        scratch_shapes=[pltpu.VMEM((ROWS * 8, HD), F32)],
        compiler_params=params(58),
        cost_estimate=cost(4 * ROWS * 8 * CTX * HD, 9 << 20),
        name="resident_attention",
    )(after, lens, query, new_kv, kv_cache)


def mix_kernel(
    after_ref, source_ref, recv_ref, conv_ref, x_ref, weight_ref, bias_ref, proj_ref,
    mixed_ref, window_ref, part_ref, send_ref,
):
    sub = iota((ROWS, 256), 0)
    lane = iota((ROWS, 256), 1)
    source = jnp.full((ROWS, 256), -1, I32)
    for r in range(ROWS):
        source = jnp.where(sub == r, source_ref[r], source)
    base = jnp.where(source >= 0, source * 8, -8)
    pick = jnp.concatenate([(lane == base + k).astype(F32) for k in range(6)], axis=0).astype(BF)
    recv = recv_ref[...].reshape(256, HALF)
    prev = jnp.dot(pick, recv, preferred_element_type=F32)
    came = source[:, 0:1] >= 0
    x = x_ref[...]
    total = x.astype(F32) * weight_ref[3:4, :].astype(F32)
    window_ref[2] = x
    for j in range(3):
        here = jnp.concatenate(
            [prev[64 * j : 64 * j + 32], prev[64 * j + 32 : 64 * j + 64]], axis=1
        )
        tap = jnp.where(came, here, conv_ref[j].astype(F32))
        if j > 0:
            window_ref[j - 1] = tap.astype(BF)
        total += tap * weight_ref[j : j + 1, :].astype(F32)
    total += bias_ref[...]
    mixed = (total / (1.0 + jnp.exp(-total))).astype(BF)
    mixed_ref[...] = mixed
    part = lax.dot_general(
        mixed, proj_ref[...], (((1,), (1,)), ((), ())), preferred_element_type=F32
    )
    part_ref[...] = part
    send_ref[...] = part.astype(BF)


def mix(after, source, recv, conv_state, x_in, weight, bias, proj_t):
    wide = proj_t.shape[0]
    return pl.pallas_call(
        mix_kernel,
        out_shape=(
            jax.ShapeDtypeStruct((ROWS, EC), BF),
            jax.ShapeDtypeStruct((3, ROWS, EC), BF),
            jax.ShapeDtypeStruct((ROWS, wide), F32),
            jax.ShapeDtypeStruct((ROWS, wide), BF),
        ),
        in_specs=[AN, SM] + [VM] * 6,
        out_specs=(VM, VM, VM, VM),
        compiler_params=ALONE,
        cost_estimate=cost(2 * ROWS * EC * wide, 4 << 20),
        name="mix_input",
    )(after, source, recv, conv_state, x_in, weight, bias, proj_t)


GROUP = 8


def advance(prev, dt, decay, drive, inject):
    return jnp.exp2(dt * decay) * prev + drive * inject


def step_kernel(*refs):
    source_ref, part_ref = refs[0:2]
    others = refs[2:9]
    (
        gain_ref, b_gain_ref, c_gain_ref, proj_ref, bias_ref, mixed_ref, skip_ref, z_ref, decay_ref, state_ref,
        dt_ref, drive_ref, inject_ref, read_ref, gate_ref, base_ref, new_ref,
        local, made, flat, in_sems, out_sems,
    ) = refs[9:]

    def fetch(r):
        return pltpu.make_async_copy(state_ref.at[r], local.at[r], in_sems.at[r])

    def store(r):
        return pltpu.make_async_copy(made.at[r], new_ref.at[r], out_sems.at[r])

    for r in range(ROWS):

        @pl.when(source_ref[r] < 0)
        def _():
            fetch(r).start()

    proj = part_ref[...]
    for other in others:
        proj += other[...].astype(F32)
    low = proj[:, 0:RANK]
    mean = jnp.sum(low * low, axis=1, keepdims=True) * (1.0 / RANK)
    normed = (low * lax.rsqrt(mean + 1e-6) * gain_ref[...]).astype(BF)
    dt = jnp.dot(normed, proj_ref[...], preferred_element_type=F32) + bias_ref[...]
    dt = jnp.maximum(dt, 0.0) + jnp.log1p(jnp.exp(-jnp.abs(dt)))
    mixed = mixed_ref[...].astype(F32)
    drive = dt * mixed
    dt = dt * (-LOG2E)
    for r in range(ROWS):
        dt_ref[r] = dt[r : r + 1, :]
        drive_ref[r] = drive[r : r + 1, :]
    z = z_ref[...].astype(F32)
    gate = z / (1.0 + jnp.exp(-z))
    gate_ref[...] = gate
    base_ref[...] = skip_ref[...] * mixed * gate
    tail = proj[:, RANK : RANK + 2 * NS]
    square = tail * tail
    front = iota((ROWS, 2 * NS), 1) < NS
    mean_b = jnp.sum(jnp.where(front, square, 0.0), axis=1, keepdims=True) * (1.0 / NS)
    mean_c = jnp.sum(jnp.where(front, 0.0, square), axis=1, keepdims=True) * (1.0 / NS)
    scale = lax.rsqrt(jnp.where(front, mean_b, mean_c) + 1e-6)
    tail_gain = jnp.concatenate([b_gain_ref[...], c_gain_ref[...]], axis=1)
    tail = (tail * scale * tail_gain).astype(BF)
    lane = iota((2 * NS, 128), 1)
    spread = (iota((2 * NS, 128), 0) == NS + lane % NS).astype(F32).astype(BF)
    read = jnp.dot(tail, spread, preferred_element_type=F32)
    own = iota((ROWS, 128), 1) // NS == iota((ROWS, 128), 0) % GROUP
    read_ref[...] = jnp.where(own, read, 0.0)
    many = (iota((ROWS * NS, ROWS), 0) // NS == iota((ROWS * NS, ROWS), 1)).astype(F32).astype(BF)
    each = jnp.dot(many, tail, preferred_element_type=F32)
    mine = iota((ROWS * NS, 2 * NS), 0) % NS == iota((ROWS * NS, 2 * NS), 1)
    each = jnp.where(mine, each, 0.0).astype(BF)
    inject = jnp.dot(each, jnp.ones((2 * NS, 128), BF), preferred_element_type=F32)
    inject_ref[...] = inject.reshape(ROWS, NS, 128)

    def body(i, carry):
        for b in range(GROUP):
            r = i * GROUP + b

            @pl.when(source_ref[r] < 0)
            def _():
                fetch(r).wait()
                inject = jnp.concatenate([inject_ref[r]] * 4, axis=1)
                for c in range(EC // 512):
                    cols = slice(c * 512, (c + 1) * 512)
                    new = advance(
                        local[r, :, cols], dt_ref[r, :, cols], decay_ref[:, cols],
                        drive_ref[r, :, cols], inject,
                    )
                    made[r, :, cols] = new
                    flat[b * NS : (b + 1) * NS, cols] = new.astype(BF)
                store(r).start()

            @pl.when(source_ref[r] >= 0)
            def _():
                flat[b * NS : (b + 1) * NS, :] = jnp.zeros((NS, EC), BF)

        rows = pl.ds(pl.multiple_of(i * GROUP, GROUP), GROUP)
        sums = jnp.dot(read_ref[rows, :].astype(BF), flat[...], preferred_element_type=F32)
        base_ref[rows, :] += sums * gate_ref[rows, :]
        return carry

    lax.fori_loop(0, ROWS // GROUP, body, 0)
    for r in range(ROWS):

        @pl.when(source_ref[r] < 0)
        def _():
            store(r).wait()


def step_size(source, part, others, *operands):
    return pl.pallas_call(
        step_kernel,
        out_shape=(
            jax.ShapeDtypeStruct((ROWS, 1, EC), F32),
            jax.ShapeDtypeStruct((ROWS, 1, EC), F32),
            jax.ShapeDtypeStruct((ROWS, NS, 128), F32),
            jax.ShapeDtypeStruct((ROWS, 128), F32),
            jax.ShapeDtypeStruct((ROWS, EC), F32),
            jax.ShapeDtypeStruct((ROWS, EC), F32),
            jax.ShapeDtypeStruct((ROWS, NS, EC), F32),
        ),
        in_specs=[SM] + [VM] * 17 + [HB],
        out_specs=(VM,) * 6 + (HB,),
        scratch_shapes=[
            pltpu.VMEM((ROWS, NS, EC), F32),
            pltpu.VMEM((ROWS, NS, EC), F32),
            pltpu.VMEM((GROUP * NS, EC), BF),
            pltpu.SemaphoreType.DMA((ROWS,)),
            pltpu.SemaphoreType.DMA((ROWS,)),
        ],
        compiler_params=params(56),
        cost_estimate=cost(2 * ROWS * EC * RANK, 12 << 20),
        name="step_and_resident",
    )(source, part, *others, *operands)


def tail_kernel(
    source_ref, came, dt_ref, drive_ref, inject_ref, read_ref, decay_ref,
    gate_ref, base_ref, mix_ref, score_ref, new_kv_ref, kept_ref,
    new_ref, out_hbm, attn_hbm,
    out_ref, attn_ref, made, flat, sums, other, pieces, sems, out_sems,
):
    def store(r):
        return pltpu.make_async_copy(made.at[r], new_ref.at[r], out_sems.at[r])

    def store_all(i):
        rows = pl.ds(pl.multiple_of(i * GROUP, GROUP), GROUP)
        return pltpu.make_async_copy(made.at[rows], new_ref.at[rows], out_sems.at[i * GROUP])

    def leave(i, act):
        count = jnp.int32(0)
        for b in range(GROUP):
            count += jnp.where(source_ref[i * GROUP + b] >= 0, 1, 0)

        @pl.when(count == GROUP)
        def _():
            act(store_all(i))

        @pl.when(count < GROUP)
        def _():
            for b in range(GROUP):
                r = i * GROUP + b

                @pl.when(source_ref[r] >= 0)
                def _():
                    act(store(r))

    lane = iota((8, HD), 1)
    huge = jnp.where(lane < 32, -NEG, 0.0)

    def body(i, carry):
        for b in range(GROUP):
            r = i * GROUP + b
            source = source_ref[r]
            here = pl.ds(pl.multiple_of(8 * r, 8), 8)

            @pl.when(source >= 0)
            def _():
                tile = came[source, :, EC:WIDE].astype(F32)
                other[here, :] = tile[0:8, :]
                pieces[here, :] = tile[8:16, :]
                inject = jnp.concatenate([inject_ref[r]] * 4, axis=1)
                for c in range(EC // 512):
                    cols = slice(c * 512, (c + 1) * 512)
                    new = advance(
                        came[source, :, cols].astype(F32), dt_ref[r, :, cols],
                        decay_ref[:, cols], drive_ref[r, :, cols], inject,
                    )
                    made[r, :, cols] = new
                    flat[b * NS : (b + 1) * NS, cols] = new.astype(BF)

            @pl.when(source < 0)
            def _():
                other[here, :] = mix_ref[here, :]
                pieces[here, :] = huge
                flat[b * NS : (b + 1) * NS, :] = jnp.zeros((NS, EC), BF)

        leave(i, lambda copy: copy.start())
        rows = pl.ds(pl.multiple_of(i * GROUP, GROUP), GROUP)
        sums[rows, :] = jnp.dot(
            read_ref[rows, :].astype(BF), flat[...], preferred_element_type=F32
        )
        return carry

    lax.fori_loop(0, ROWS // GROUP, body, 0)
    out_ref[...] = (sums[...] * gate_ref[...] + base_ref[...]).astype(BF)
    give_out = pltpu.make_async_copy(out_ref, out_hbm, sems.at[0])
    give_out.start()
    lse = pieces[:, 0:1] + pieces[:, 32:33] + pieces[:, 64:65]
    score = score_ref[...]
    peak = jnp.maximum(lse, score)
    old = jnp.exp(lse - peak)
    new = jnp.exp(score - peak)
    value = new_kv_ref[:, HD:].astype(F32)
    value = jnp.concatenate(
        [jnp.broadcast_to(value[r : r + 1, :], (8, HD)) for r in range(ROWS)], axis=0
    )
    pieces[...] = (other[...] * old + new * value) / (old + new)
    for h in range(HEADS):
        attn_ref[:, h * HD : (h + 1) * HD] = pieces[pl.ds(h, ROWS, 8), :].astype(BF)
    give_attn = pltpu.make_async_copy(attn_ref, attn_hbm, sems.at[1])
    give_attn.start()
    give_out.wait()
    give_attn.wait()
    for i in range(ROWS // GROUP):
        leave(i, lambda copy: copy.wait())


def tail(*operands):
    return pl.pallas_call(
        tail_kernel,
        out_shape=(
            jax.ShapeDtypeStruct((ROWS, NS, EC), F32),
            jax.ShapeDtypeStruct((ROWS, EC), BF),
            jax.ShapeDtypeStruct((ROWS, HEADS * HD), BF),
        ),
        in_specs=[SM] + [VM] * 11 + [AN],
        out_specs=(AN, HB, HB),
        input_output_aliases={12: 0},
        scratch_shapes=[
            pltpu.VMEM((ROWS, EC), BF),
            pltpu.VMEM((ROWS, HEADS * HD), BF),
            pltpu.VMEM((ROWS, NS, EC), F32),
            pltpu.VMEM((GROUP * NS, EC), BF),
            pltpu.VMEM((ROWS, EC), F32),
            pltpu.VMEM((ROWS * 8, HD), F32),
            pltpu.VMEM((ROWS * 8, HD), F32),
            pltpu.SemaphoreType.DMA((10,)),
            pltpu.SemaphoreType.DMA((ROWS,)),
        ],
        compiler_params=ALONE,
        cost_estimate=cost(16 << 20, 8 << 20),
        name="update_and_join",
    )(*operands)


def swap(values, order):
    return lax.all_to_all(
        values, "rep", split_axis=0, concat_axis=0, tiled=True, axis_index_groups=[order]
    )


def shards(
    x_in, z_gate, conv_state, conv_pool, ssm_state, ssm_pool, conv_weight, conv_bias, x_proj,
    dt_gain, b_gain, c_gain, dt_proj, dt_bias, decay_rate, skip, query, new_kv, kv_cache, kv_pool,
    ctx_len, row_owner, row_pos, swap_slot, swap_lens, swap_pages,
):
    slots = swap_slot.transpose(0, 2, 1)
    firsts = [first_peer(p) for p in range(PEERS)]
    seconds = [second_peer(p) for p in range(PEERS)]
    first = swap(pack(slots, row_owner, row_pos, conv_pool.transpose(1, 0, 2), query), firsts)
    states, bias, rest, source, state_source = prepare(
        slots, row_owner, row_pos, swap_pages, swap_lens.transpose(0, 2, 1), ssm_pool
    )
    states = serve(first, bias, rest, kv_pool, states)
    second = swap(states.reshape(PEERS, CAP * NS, WIDE), seconds).reshape(ENT, NS, WIDE)

    mixed, window, part, send = mix(
        states, source, first, conv_state.transpose(1, 0, 2), x_in, conv_weight,
        conv_bias.reshape(1, EC), x_proj.T,
    )
    tp = lax.axis_size("tp")
    others = [
        lax.ppermute(send, "tp", [(i, (i + s) % tp) for i in range(tp)]) for s in range(1, tp)
    ]
    mix_here, score = resident(states, ctx_len, query, new_kv, kv_cache)
    dt, drive, inject, read, gate, base, kept = step_size(
        state_source, part, others, dt_gain.reshape(1, RANK),
        b_gain.reshape(1, NS), c_gain.reshape(1, NS), dt_proj, dt_bias.reshape(1, EC), mixed,
        skip.reshape(1, EC), z_gate, decay_rate, ssm_state,
    )
    new_ssm, mamba_out, attn_out = tail(
        state_source, second, dt, drive, inject, read, decay_rate, gate, base, mix_here, score, new_kv, kept
    )
    return (mamba_out, attn_out, new_ssm, window.transpose(1, 0, 2))


def solution(mesh):
    in_specs = (
        P("rep", "tp"), P("rep", "tp"), P("rep", None, "tp"), P("rep", None, "tp"),
        P("rep", None, "tp"), P("rep", None, "tp"), P(None, "tp"), P("tp"), P("tp", None),
        P(), P(), P(), P(None, "tp"), P("tp"), P(None, "tp"), P("tp"), P("rep", "tp"),
        P("rep", "tp"), P("rep", None, "tp"), P("rep", None, "tp"), P("rep"), P("rep"), P("rep"),
        P("rep", None, None), P("rep", None, None), P("rep", None, None, None),
    )
    out_specs = (P("rep", "tp"), P("rep", "tp"), P("rep", None, "tp"), P("rep", None, "tp"))
    return jax.shard_map(shards, mesh=mesh, in_specs=in_specs, out_specs=out_specs, check_vma=False)
```
